256 devices in a mesh: tile: 64 (over y, z_hi, x, core), batch: 4 (over z_lo).
Axes of the slice: x: 4, y: 4, z: 8 (z_hi: 2, z_lo: 4; z = z_hi * 4 + z_lo), core: 2. Of those that a mesh axis runs over, the one named last changes fastest.
Arguments:
- object_tiles: float32 [64, 2, 384, 384], P('tile'), may hold values from -5 to 5
- probe: bfloat16 [8, 2, 256, 256], replicated, may hold values from -4 to 4
- offsets: int32 [64, 4, 2], P('tile', 'batch'), may hold values from 0 to 383, as said below
- amplitude: float32 [64, 4, 256, 256], P('tile', 'batch'), may hold values from 0.3 to 3
Outputs:
- object_grad: float32 [64, 2, 384, 384], P('tile')
- probe_grad: float32 [8, 2, 256, 256], replicated
The draws below stay inside these ranges and needn't reach their ends.
Inputs may be any that keep to these rules, and one draw needn't show every extreme that they name: `offsets`: offsets are such that every patch lies inside the region: in tiles of the last tile row the row offset is at most 128, in tiles of the last tile column the column offset likewise.
All inputs are finite; a program needn't handle non-finite values.
Results may differ from the reference program's by a relative error of at most 0.0003.
Values sent between devices are 32-bit elements; how exact they have to be, the bound alone decides.
No kernel may reach another device: no remote copies, remote signals or barrier semaphores. Data moves between devices by JAX's collectives and lax.ppermute only.
A program may use at most 64 MiB of HBM per device.

```python
import math
import jax
import jax.numpy as jnp
from jax import lax

MODES = 8
P_SIZE = 256
TS = 384
TILE_COLS = 4
TILES = 64
POS_TILE = 4
POSITIONS = 256


def draw_offsets(key, part):
    key = jax.random.fold_in(key, 11)
    tile_ids = jnp.arange(TILES, dtype=jnp.int32)
    last_row = tile_ids // TILE_COLS == TILES // TILE_COLS - 1
    last_col = tile_ids % TILE_COLS == TILE_COLS - 1
    limit_y = jnp.where(last_row, TS - P_SIZE + 1, TS)
    limit_x = jnp.where(last_col, TS - P_SIZE + 1, TS)
    limits = jnp.stack([limit_y, limit_x], axis=-1)[:, None, :]
    limits = jnp.broadcast_to(limits, (TILES, POS_TILE, 2)).astype(jnp.int32)
    drawn = jax.random.randint(key, (TILES, POS_TILE, 2), 0, limits, dtype=jnp.int32)
    drawn = drawn.at[0, 0, :].set(TS - 1)
    drawn = drawn.at[0, 1, :].set(0)
    return drawn.astype(jnp.int32)


def block_levels(stream_key, shape, pieces, smallest, top_value):
    factor_of, own = 1.0, jax.random.fold_in(stream_key, 6)
    for axis_at, blocks in pieces:
        draws = jnp.exp(jax.random.uniform(jax.random.fold_in(own, axis_at), (blocks,), jnp.float32, smallest / len(pieces), top_value / len(pieces)))
        factor_of = factor_of * jnp.repeat(draws, shape[axis_at] // blocks).reshape([-1 if axis == axis_at else 1 for axis in range(len(shape))])
    return factor_of


def bell_draw(rng, shape, scale, limit, pieces=(), held_as=jnp.bfloat16):
    values = scale * jax.random.normal(rng, shape, jnp.float32)
    if pieces:
        values = values * block_levels(rng, shape, pieces, -0.22, 0.18)
    return jnp.clip(values, -limit, limit).astype(held_as)


def setup_inputs(seed: int = 0) -> dict:
    streams_of = jax.random.split(jax.random.key(seed), 5)
    return {
        "object_tiles": bell_draw(streams_of[0], (TILES, 2, TS, TS), 0.7, 5.0, ((0, 64),), jnp.float32),
        "probe": bell_draw(streams_of[1], (MODES, 2, P_SIZE, P_SIZE), 0.5, 4.0),
        "offsets": draw_offsets(jax.random.fold_in(streams_of[4], 71), 0),
        "amplitude": jnp.clip(jnp.exp(math.log(3.0) - 2.3025851 * jax.random.uniform(streams_of[3], (TILES, POS_TILE, P_SIZE, P_SIZE), jnp.float32) ** block_levels(streams_of[3], (TILES, POS_TILE, P_SIZE, P_SIZE), ((0, 64), (1, 4)), -0.2, 0.2)), 0.3, 3.0),
    }


def reference(object_tiles, probe, offsets, amplitude):
    tile_rows = TILES // TILE_COLS
    region = object_tiles.reshape(tile_rows, TILE_COLS, 2, TS, TS).transpose(2, 0, 3, 1, 4)
    region = region.reshape(2, tile_rows * TS, TILE_COLS * TS)
    region = jnp.pad(region, ((0, 0), (0, P_SIZE), (0, P_SIZE)))
    tile_ids = jnp.arange(TILES, dtype=jnp.int32)
    base_y = tile_ids // TILE_COLS * TS
    base_x = tile_ids % TILE_COLS * TS
    glob_y = (base_y[:, None] + offsets[:, :, 0]).reshape(-1).astype(jnp.int32)
    glob_x = (base_x[:, None] + offsets[:, :, 1]).reshape(-1).astype(jnp.int32)
    measured = amplitude.reshape(-1, P_SIZE, P_SIZE)
    probe_wide = probe.astype(jnp.float32)
    probe_cplx = probe_wide[:, 0] + 1j * probe_wide[:, 1]
    zero_index = jnp.int32(0)

    def advance(totals, sample):
        grad_region, grad_probe = totals
        row_at, col_at, target = sample
        object_patch = lax.dynamic_slice(region, (zero_index, row_at, col_at), (2, P_SIZE, P_SIZE))
        patch_cplx = object_patch[0] + 1j * object_patch[1]
        far_field = jnp.fft.fft2(probe_cplx * patch_cplx[None], norm='ortho')
        intensity = lax.optimization_barrier(jnp.sum(jnp.real(far_field) ** 2 + jnp.imag(far_field) ** 2, axis=0))
        corrected = far_field * (1.0 - target / jnp.sqrt(intensity + 0.01))[None]
        back_wave = jnp.fft.ifft2(corrected, norm='ortho')
        object_term = lax.optimization_barrier(jnp.sum(jnp.conj(probe_cplx) * back_wave, axis=0))
        old_values = lax.dynamic_slice(grad_region, (zero_index, row_at, col_at), (2, P_SIZE, P_SIZE))
        new_values = old_values + jnp.stack([jnp.real(object_term), jnp.imag(object_term)])
        grad_region = lax.dynamic_update_slice(grad_region, new_values, (zero_index, row_at, col_at))
        grad_probe = grad_probe + jnp.conj(patch_cplx)[None] * back_wave
        return ((grad_region, grad_probe), None)
    start_region = jnp.zeros_like(region)
    start_probe = jnp.zeros_like(probe_cplx)
    (grad_region, grad_probe), _ = lax.scan(advance, (start_region, start_probe), (glob_y, glob_x, measured))
    grad_region = grad_region[:, :tile_rows * TS, :TILE_COLS * TS]
    object_grad = grad_region.reshape(2, tile_rows, TS, TILE_COLS, TS).transpose(1, 3, 0, 2, 4).reshape(TILES, 2, TS, TS)
    probe_grad = jnp.stack([jnp.real(grad_probe), jnp.imag(grad_probe)], axis=1) / jnp.sqrt(jnp.float32(POSITIONS))
    return (object_grad, probe_grad)
```

```python
import math

import jax
import jax.numpy as jnp
from jax import lax
from jax.sharding import Mesh, PartitionSpec as P

TILE_COLS = 4
AXES = ("y", "zh", "x", "core", "zl")
SIZES = (4, 2, 4, 2, 4)
TILE_AXES = AXES[:4]
GROUPS = 4
ROW_BLOCK = 8


def dft_blocks(pattern):
    counter = jnp.arange(pattern, dtype=jnp.int32)
    phase_index = counter[:, None] * counter[None, :] % pattern
    angles = phase_index.astype(jnp.float32) * (2.0 * math.pi / pattern)
    cosine = jnp.cos(angles) / math.sqrt(pattern)
    sine_table = jnp.sin(angles) / math.sqrt(pattern)
    first_table = jnp.stack(
        [jnp.stack([cosine, sine_table], axis=1), jnp.stack([-sine_table, cosine], axis=1)], axis=0
    )
    second_table = jnp.stack(
        [jnp.stack([cosine, -sine_table], axis=1), jnp.stack([sine_table, cosine], axis=1)], axis=0
    )
    return (first_table, second_table)


def transform(wave, left_table, right_table):
    half_done = jnp.einsum("ajbk,mbkc->majc", left_table, wave, precision=lax.Precision.HIGH)
    return jnp.einsum("mbjk,bkac->majc", half_done, right_table, precision=lax.Precision.HIGH)


def mirrored(tile, group):
    z_hi = tile // 8 % 2
    return group if z_hi == 0 else GROUPS - 1 - group


def across_columns(block, step):
    route = [(t, t + step) for t in range(64) if 0 <= t % TILE_COLS + step < TILE_COLS]
    return lax.ppermute(block, TILE_AXES, route)


def across_rows(block, step):
    route = []
    for t in range(64):
        u = t + step * TILE_COLS
        if 0 <= u < 64:
            for k in range(GROUPS):
                route.append((t * GROUPS + mirrored(t, k), u * GROUPS + mirrored(u, k)))
    return lax.ppermute(block, AXES, route)


def among(block, axis, distance):
    n = lax.axis_size(axis)
    return lax.ppermute(block, axis, [(i, i ^ distance) for i in range(n)])


def pick(stack, index, axis=0):
    return lax.dynamic_index_in_dim(stack, index, axis, keepdims=False)


def scatter_sum(parts, axis):
    me = lax.axis_index(axis)
    total = pick(parts, me)
    arrived = [among(pick(parts, me ^ d), axis, d) for d in (1, 2, 3)]
    return total + (arrived[0] + (arrived[1] + arrived[2]))


def by_place(pieces, me):
    one, two = me % 2 == 1, me // 2 == 1
    pairs = [(jnp.where(one, b, a), jnp.where(one, a, b)) for a, b in (pieces[:2], pieces[2:])]
    low = [jnp.where(two, q, p) for p, q in zip(*pairs)]
    high = [jnp.where(two, p, q) for p, q in zip(*pairs)]
    return jnp.stack(low + high)


def gathered(part, axis):
    me = lax.axis_index(axis)
    return by_place([part] + [among(part, axis, d) for d in (1, 2, 3)], me)


def probe_sum(grad_probe):
    shape = grad_probe.shape
    core = lax.axis_index("core")
    halves = grad_probe.reshape(2, 2, 4, 4, 8, 8, 256)
    half = pick(halves, core) + among(pick(halves, 1 - core), "core", 1)
    first = scatter_sum(half[0], "x")
    second = scatter_sum(half[1], "y")
    first = scatter_sum(first, "y")
    second = scatter_sum(second, "x")
    mine = jnp.stack([first, second], axis=1)
    spread = lax.all_to_all(mine, ("zh", "zl"), 0, 0, tiled=True)
    total = jnp.sum(spread, axis=0) * (1.0 / 16.0)
    spread = jnp.broadcast_to(total[None], (8,) + total.shape)
    whole = lax.all_to_all(spread, ("zh", "zl"), 0, 0, tiled=True)
    first = gathered(whole[:, 0], "y")
    second = gathered(whole[:, 1], "x")
    half = jnp.stack([gathered(first, "x"), gathered(second, "y")])
    other = among(half, "core", 1)
    return jnp.where(core == 0, jnp.stack([half, other]), jnp.stack([other, half])).reshape(shape)


def shards(object_tiles, probe, offsets, amplitude):
    own_tile = object_tiles[0]
    pattern = probe.shape[-1]
    tile_side = own_tile.shape[-1]
    zero = jnp.int32(0)
    place = offsets[0, 0]
    row_at, col_at = place[0], place[1]
    z_hi, z_lo = lax.axis_index("zh"), lax.axis_index("zl")
    row_class = jnp.where(z_hi == 0, z_lo, GROUPS - 1 - z_lo)

    place_above = across_rows(place, 1)
    widened = jnp.concatenate([own_tile, across_columns(own_tile[:, :, :pattern], -1)], axis=2)
    frame = lax.dynamic_slice(widened, (zero, zero, place_above[1]), (2, pattern, pattern))
    below = across_rows(frame, -1)
    above = lax.dynamic_slice(widened, (zero, zero, col_at), (2, tile_side, pattern))
    object_patch = lax.dynamic_slice(
        jnp.concatenate([above, below], axis=1), (zero, row_at, zero), (2, pattern, pattern)
    )
    places = [place] + [among(place, "zl", d) for d in (1, 2, 3)]

    first_table, second_table = dft_blocks(pattern)
    probe_wide = probe.astype(jnp.float32)
    probe_re = probe_wide[:, 0]
    probe_im = probe_wide[:, 1]
    exit_wave = jnp.stack(
        [
            probe_re * object_patch[0] - probe_im * object_patch[1],
            probe_re * object_patch[1] + probe_im * object_patch[0],
        ],
        axis=1,
    )
    far_field = transform(exit_wave, first_table, second_table)
    intensity = jnp.sum(far_field * far_field, axis=(0, 1))
    factor = 1.0 - amplitude[0, 0] / jnp.sqrt(intensity + 0.01)
    back_wave = transform(far_field * factor, second_table, first_table)
    back_re = back_wave[:, 0]
    back_im = back_wave[:, 1]
    object_term = jnp.stack(
        [
            jnp.sum(probe_re * back_re + probe_im * back_im, axis=0),
            jnp.sum(probe_re * back_im - probe_im * back_re, axis=0),
        ]
    )
    grad_probe = jnp.stack(
        [
            object_patch[0] * back_re + object_patch[1] * back_im,
            object_patch[0] * back_im - object_patch[1] * back_re,
        ],
        axis=1,
    )

    framed = jnp.zeros((2, 288, pattern), jnp.float32)
    framed = lax.dynamic_update_slice(framed, object_term, (zero, row_at % ROW_BLOCK, zero))
    framed = framed.reshape(2, 9, GROUPS, ROW_BLOCK, pattern)
    kept = None
    arrived = []
    for d in range(GROUPS):
        group = row_class ^ d
        rows = pick(framed, (group - row_at // ROW_BLOCK) % GROUPS, axis=2)
        arrived.append(rows if d == 0 else among(rows, "zl", d))
    owned = jnp.zeros((2, 21, ROW_BLOCK, tile_side + pattern), jnp.float32)
    for rows, spot in zip(arrived, places):
        block = spot[0] // ROW_BLOCK
        start = (block + (row_class - block) % GROUPS) // GROUPS
        spots = (zero, start, zero, spot[1])
        owned = lax.dynamic_update_slice(owned, lax.dynamic_slice(owned, spots, rows.shape) + rows, spots)
    owned = owned[:, :20]
    from_left = across_columns(owned[:, :, :, tile_side:], 1)
    owned = owned[:, :, :, :tile_side].at[:, :, :, :pattern].add(from_left)
    from_above = across_rows(owned[:, 12:], 1)
    owned = owned[:, :12].at[:, :8].add(from_above)
    pieces = [owned] + [among(owned, "zl", d) for d in (1, 2, 3)]
    object_grad = by_place(pieces, row_class)
    object_grad = object_grad.transpose(1, 2, 0, 3, 4).reshape(2, tile_side, tile_side)
    return (object_grad[None], probe_sum(grad_probe))


def solution(mesh):
    fine = Mesh(mesh.devices.reshape(SIZES), AXES)
    placed = (
        P(TILE_AXES, None, None, None),
        P(),
        P(TILE_AXES, "zl", None),
        P(TILE_AXES, "zl", None, None),
    )
    return jax.shard_map(
        shards,
        mesh=fine,
        in_specs=placed,
        out_specs=(P(TILE_AXES, None, None, None), P()),
        check_vma=False,
    )
```

```python
import math

import jax
import jax.numpy as jnp
import ml_dtypes
import numpy as np
from jax import lax
from jax.experimental import pallas as pl
from jax.experimental.pallas import tpu as pltpu
from jax.sharding import Mesh, PartitionSpec as P

GROUPS = 4
ROW_BLOCK = 8
BF16 = jnp.bfloat16
F32 = jnp.float32
VMEM_LIMIT = 48 * 1024 * 1024


def split_table(table):
    high = table.astype(ml_dtypes.bfloat16)
    low = (table - high.astype(np.float64)).astype(ml_dtypes.bfloat16)
    return high, low


def dft_tables(pattern):
    half = pattern // 2
    angles = 2.0 * np.pi / half * (np.outer(np.arange(half), np.arange(half)) % half)
    cosine, sine = np.cos(angles) / math.sqrt(pattern), np.sin(angles) / math.sqrt(pattern)
    table = np.block([[cosine, -sine], [sine, cosine]])
    high, low = split_table(table)
    down = np.concatenate([high, high, low], axis=0)
    across = np.concatenate([high, high, low], axis=1)
    turned = [np.ascontiguousarray(part.T) for part in (high, low)]
    down_t = np.concatenate([turned[0], turned[0], turned[1]], axis=0)
    across_t = np.concatenate([turned[0], turned[0], turned[1]], axis=1)
    twist = 2.0 * np.pi / pattern * np.arange(half)
    lanes = np.stack([np.cos(twist), -np.sin(twist)])[:, None, :].astype(np.float32)
    rows = np.ascontiguousarray(
        np.broadcast_to(np.stack([np.cos(twist), -np.sin(twist)])[:, :, None], (2, half, half))
    ).astype(np.float32)
    return down, across, down_t, across_t, lanes, rows


def parts(x):
    high = x.astype(BF16)
    return high, (x - high.astype(F32)).astype(BF16)


def times(x, table):
    high, low = parts(x)
    return jnp.dot(jnp.concatenate([high, low, high], axis=1), table, preferred_element_type=F32)


def under(table, x):
    high, low = parts(x)
    return jnp.dot(table, jnp.concatenate([high, low, high], axis=0), preferred_element_type=F32)


def forward(re, im, down, across_t, lanes, rows):
    h = re.shape[0] // 2
    wr, wi = lanes
    a, b, c, d = re[:, :h], re[:, h:], im[:, :h], im[:, h:]
    p, q = a - b, c - d
    even = times(jnp.concatenate([a + b, c + d], axis=1), down)
    odd = times(jnp.concatenate([p * wr - q * wi, p * wi + q * wr], axis=1), down)
    re = jnp.concatenate([even[:, :h], odd[:, :h]], axis=1)
    im = jnp.concatenate([even[:, h:], odd[:, h:]], axis=1)
    wr, wi = rows
    a, b, c, d = re[:h], re[h:], im[:h], im[h:]
    p, q = a - b, c - d
    even = under(across_t, jnp.concatenate([a + b, c + d], axis=0))
    odd = under(across_t, jnp.concatenate([p * wr - q * wi, p * wi + q * wr], axis=0))
    return jnp.concatenate([even[:h], odd[:h]], axis=0), jnp.concatenate([even[h:], odd[h:]], axis=0)


def backward(re, im, down_t, across, lanes, rows):
    h = re.shape[0] // 2
    wr, wi = rows
    even = under(across, jnp.concatenate([re[:h], im[:h]], axis=0))
    odd = under(across, jnp.concatenate([re[h:], im[h:]], axis=0))
    p, q = odd[:h], odd[h:]
    p, q = p * wr + q * wi, q * wr - p * wi
    re = jnp.concatenate([even[:h] + p, even[:h] - p], axis=0)
    im = jnp.concatenate([even[h:] + q, even[h:] - q], axis=0)
    wr, wi = lanes
    even = times(jnp.concatenate([re[:, :h], im[:, :h]], axis=1), down_t)
    odd = times(jnp.concatenate([re[:, h:], im[:, h:]], axis=1), down_t)
    p, q = odd[:, :h], odd[:, h:]
    p, q = p * wr + q * wi, q * wr - p * wi
    re = jnp.concatenate([even[:, :h] + p, even[:, :h] - p], axis=1)
    im = jnp.concatenate([even[:, h:] + q, even[:, h:] - q], axis=1)
    return re, im


def twiddles(lanes_ref, rows_ref):
    rows = [jnp.concatenate([rows_ref[i], rows_ref[i]], axis=1) for i in range(2)]
    return (lanes_ref[0], lanes_ref[1]), rows


def gradients(re, im, m, i, patch_ref, probe_ref, term, grad_ref, tables):
    re, im = backward(re, im, *tables)
    grad_ref[i, 0] = patch_ref[0] * re + patch_ref[1] * im
    grad_ref[i, 1] = patch_ref[0] * im - patch_ref[1] * re
    probe_re, probe_im = probe_ref[m, 0].astype(F32), probe_ref[m, 1].astype(F32)
    term[0] += probe_re * re + probe_im * im
    term[1] += probe_re * im - probe_im * re


def first_kernel(
    where_ref, rows0, rows1, rows2, rows3, probe_ref, amplitude_ref, down, across, down_t, across_t, lanes_ref, rows_ref,
    sent_ref, corrected_ref, patch_ref, term_ref, frame, far, total,
):
    pattern = amplitude_ref.shape[0]
    modes = probe_ref.shape[0]
    half = modes // 2
    row_at, core, other_turn = where_ref[0], where_ref[1], where_ref[4]
    turn = where_ref[3]
    block, shift = row_at // ROW_BLOCK, row_at % ROW_BLOCK
    count = frame.shape[1]
    for d, rows in enumerate((rows0, rows1, rows2, rows3)):
        first = ((where_ref[2] ^ d) + GROUPS - block % GROUPS) % GROUPS
        for i in range(count // GROUPS):
            frame[:, first + GROUPS * i] = rows[:, i]
    height = pattern + ROW_BLOCK
    for channel in range(2):
        window = frame[channel, : count - 3].reshape(height, pattern)
        patch_ref[channel] = pltpu.roll(window, (height - shift) % height, 0)[:pattern]
    lanes, rows = twiddles(lanes_ref, rows_ref)
    total[...] = jnp.full_like(total, 0.01)

    def outward(m, carry):
        probe_re, probe_im = probe_ref[m, 0].astype(F32), probe_ref[m, 1].astype(F32)
        re = probe_re * patch_ref[0] - probe_im * patch_ref[1]
        im = probe_re * patch_ref[1] + probe_im * patch_ref[0]
        re, im = forward(re, im, down[...], across_t[...], lanes, rows)
        far[m, 0] = re
        far[m, 1] = im
        total[...] += re * re + im * im
        return carry

    lax.fori_loop(0, modes, outward, 0, unroll=UNROLL)
    total[...] = 1.0 - amplitude_ref[...] * lax.rsqrt(total[...])
    term_ref[...] = jnp.zeros_like(term_ref)
    tables = (down_t[...], across[...], lanes, rows)

    def homeward(i, carry):
        m = (1 - core) * half + (other_turn ^ i)
        kept = core * half + (turn ^ i)
        corrected_ref[i, 0] = far[kept, 0] * total[...]
        corrected_ref[i, 1] = far[kept, 1] * total[...]
        gradients(far[m, 0] * total[...], far[m, 1] * total[...], m, i, patch_ref, probe_ref, term_ref, sent_ref, tables)
        return carry

    lax.fori_loop(0, half, homeward, 0, unroll=UNROLL)


def second_kernel(
    where_ref, corrected_ref, patch_ref, term_ref, probe_ref, across, down_t, lanes_ref, rows_ref,
    kept_ref, rows0, rows1, rows2, rows3, term, frame,
):
    pattern = patch_ref.shape[1]
    half = corrected_ref.shape[0]
    row_at, core, row_class, turn = where_ref[0], where_ref[1], where_ref[2], where_ref[3]
    lanes, rows = twiddles(lanes_ref, rows_ref)
    tables = (down_t[...], across[...], lanes, rows)
    term[...] = term_ref[...]

    def homeward(i, carry):
        gradients(
            corrected_ref[i, 0],
            corrected_ref[i, 1],
            core * half + (turn ^ i),
            i,
            patch_ref,
            probe_ref,
            term,
            kept_ref,
            tables,
        )
        return carry

    lax.fori_loop(0, half, homeward, 0, unroll=UNROLL)
    block = row_at // ROW_BLOCK
    shift = row_at % ROW_BLOCK
    count = frame.shape[1]
    for channel in range(2):
        padded = jnp.concatenate([term[channel], jnp.zeros((ROW_BLOCK, pattern), F32)], axis=0)
        frame[channel, : count - 3] = pltpu.roll(padded, shift, 0).reshape(count - 3, ROW_BLOCK, pattern)
        frame[channel, count - 3 :] = jnp.zeros((3, ROW_BLOCK, pattern), F32)
    for d, out in enumerate((rows0, rows1, rows2, rows3)):
        first = ((row_class ^ d) + GROUPS - block % GROUPS) % GROUPS
        for i in range(count // GROUPS):
            out[:, i] = frame[:, first + GROUPS * i]


def whole(space=pltpu.VMEM):
    return pl.BlockSpec(memory_space=space)


UNROLL = 2


def first_call(where, pieces, probe, amplitude, tables):
    modes, _, pattern, _ = probe.shape
    half = (modes // 2, 2, pattern, pattern)
    shapes = [half, half, (2, pattern, pattern), (2, pattern, pattern)]
    return pl.pallas_call(
        first_kernel,
        out_shape=[jax.ShapeDtypeStruct(s, F32) for s in shapes],
        in_specs=[whole(pltpu.SMEM)] + [whole()] * 12,
        out_specs=[whole()] * 4,
        scratch_shapes=[
            pltpu.VMEM((2, pattern // ROW_BLOCK + GROUPS, ROW_BLOCK, pattern), F32),
            pltpu.VMEM((modes, 2, pattern, pattern), F32),
            pltpu.VMEM((pattern, pattern), F32),
        ],
        compiler_params=pltpu.CompilerParams(vmem_limit_bytes=VMEM_LIMIT),
        name="outward",
    )(where, *pieces, probe, amplitude, *tables)


def second_call(where, corrected, patch, term, probe, tables):
    down, across, down_t, across_t, lanes, rows = tables
    pattern = patch.shape[1]
    blocks = pattern // ROW_BLOCK + GROUPS
    piece = (2, blocks // GROUPS, ROW_BLOCK, pattern)
    shapes = [corrected.shape] + [piece] * GROUPS
    return pl.pallas_call(
        second_kernel,
        out_shape=[jax.ShapeDtypeStruct(s, F32) for s in shapes],
        in_specs=[whole(pltpu.SMEM)] + [whole()] * 8,
        out_specs=[whole()] * 5,
        scratch_shapes=[
            pltpu.VMEM((2, pattern, pattern), F32),
            pltpu.VMEM((2, blocks, ROW_BLOCK, pattern), F32),
        ],
        compiler_params=pltpu.CompilerParams(vmem_limit_bytes=VMEM_LIMIT),
        name="homeward",
    )(where, corrected, patch, term, probe, across, down_t, lanes, rows)


def class_start(spot, row_class):
    block = spot[0] // ROW_BLOCK
    start = (block + (row_class + GROUPS - block % GROUPS) % GROUPS) // GROUPS
    return pl.multiple_of(start * ROW_BLOCK, ROW_BLOCK)


def cut_kernel(
    class_ref, spot0, spot1, spot2, spot3, tile_ref, right_ref, low_ref, corner_ref, rows0, rows1, rows2, rows3, owned
):
    row_class = class_ref[0]
    _, blocks, _, _, side = tile_ref.shape
    inside = blocks * ROW_BLOCK
    _, outside, _ = low_ref.shape
    for i in range(blocks):
        owned[:, ROW_BLOCK * i : ROW_BLOCK * (i + 1), :side] = tile_ref[:, i, row_class]
    owned[:, :inside, side:] = right_ref[...]
    owned[:, inside : inside + outside, :side] = low_ref[...]
    owned[:, inside : inside + outside, side:] = corner_ref[...]
    owned[:, inside + outside :] = jnp.zeros((2, ROW_BLOCK, owned.shape[2]), F32)
    for spot, rows in ((spot0, rows0), (spot1, rows1), (spot2, rows2), (spot3, rows3)):
        _, count, _, width = rows.shape
        col_at = spot[1]
        down = pl.ds(class_start(spot, row_class), count * ROW_BLOCK)
        across = pl.ds(pl.multiple_of(col_at // 128 * 128, 128), width + 128)
        for channel in range(2):
            wide = pltpu.roll(owned[channel, down, across], (width + 128 - col_at % 128) % (width + 128), 1)
            rows[channel] = wide[:, :width].reshape(count, ROW_BLOCK, width)


def cut_call(row_class, spots, tile, right, low, corner):
    _, blocks, _, _, side = tile.shape
    width = right.shape[2]
    piece = (2, (width // ROW_BLOCK + GROUPS) // GROUPS, ROW_BLOCK, width)
    return pl.pallas_call(
        cut_kernel,
        out_shape=[jax.ShapeDtypeStruct(piece, F32)] * GROUPS,
        in_specs=[whole(pltpu.SMEM)] * 5 + [whole()] * 4,
        out_specs=[whole()] * GROUPS,
        scratch_shapes=[pltpu.VMEM((2, (side + width) // GROUPS + ROW_BLOCK, side + width), F32)],
        compiler_params=pltpu.CompilerParams(vmem_limit_bytes=VMEM_LIMIT),
        name="cut",
    )(row_class, *spots, tile, right, low, corner)


def place_kernel(class_ref, spot0, spot1, spot2, spot3, rows0, rows1, rows2, rows3, body_ref, margin_ref, owned):
    row_class = class_ref[0]
    owned[...] = jnp.zeros_like(owned)
    for spot, rows in ((spot0, rows0), (spot1, rows1), (spot2, rows2), (spot3, rows3)):
        _, count, _, width = rows.shape
        col_at = spot[1]
        down = pl.ds(class_start(spot, row_class), count * ROW_BLOCK)
        across = pl.ds(pl.multiple_of(col_at // 128 * 128, 128), width + 128)
        for channel in range(2):
            block_rows = rows[channel].reshape(count * ROW_BLOCK, width)
            wide = jnp.concatenate([block_rows, jnp.zeros((count * ROW_BLOCK, 128), F32)], axis=1)
            owned[channel, down, across] += pltpu.roll(wide, col_at % 128, 1)
    height, side = body_ref.shape[1:]
    body_ref[...] = owned[:, :height, :side]
    margin_ref[...] = owned[:, :height, side:]


def place_call(row_class, spots, pieces, side):
    _, count, _, width = pieces[0].shape
    height = (side + width) // GROUPS
    return pl.pallas_call(
        place_kernel,
        out_shape=[jax.ShapeDtypeStruct((2, height, w), F32) for w in (side, width)],
        in_specs=[whole(pltpu.SMEM)] * 5 + [whole()] * 4,
        out_specs=[whole()] * 2,
        scratch_shapes=[pltpu.VMEM((2, height + ROW_BLOCK, side + width), F32)],
        compiler_params=pltpu.CompilerParams(vmem_limit_bytes=VMEM_LIMIT),
        name="place",
    )(row_class, *spots, *pieces)


def join_kernel(class_ref, rows0, rows1, rows2, rows3, out_ref):
    for d, rows in enumerate((rows0, rows1, rows2, rows3)):
        place = class_ref[0] ^ d
        for i in range(out_ref.shape[1]):
            out_ref[:, i, place] = rows[:, ROW_BLOCK * i : ROW_BLOCK * (i + 1)]


def join_call(row_class, pieces):
    _, height, side = pieces[0].shape
    out = pl.pallas_call(
        join_kernel,
        out_shape=jax.ShapeDtypeStruct((2, height // ROW_BLOCK, GROUPS, ROW_BLOCK, side), F32),
        in_specs=[whole(pltpu.SMEM)] + [whole()] * 4,
        out_specs=whole(),
        compiler_params=pltpu.CompilerParams(vmem_limit_bytes=VMEM_LIMIT),
        name="join",
    )(row_class, *pieces)
    return out.reshape(1, 2, height * GROUPS, side)


def fill_kernel(where_ref, *refs):
    count = (len(refs) - 2) // 2
    pieces, out_ref, sems = refs[: 2 * count], refs[-2], refs[-1]
    core, turns = where_ref[1], (where_ref[3], where_ref[4])
    copies = []
    for n, piece in enumerate(pieces):
        side, d = n // count, n % count
        slot = count * (core ^ side) + (turns[side] ^ d)
        copies.append(pltpu.make_async_copy(piece, out_ref.at[slot], sems.at[n]))
    for copy in copies:
        copy.start()
    for copy in copies:
        copy.wait()


def fill_call(where, pieces, shape):
    pieces = [piece.reshape(shape[1:]) for piece in pieces]
    return pl.pallas_call(
        fill_kernel,
        out_shape=jax.ShapeDtypeStruct(shape, F32),
        in_specs=[whole(pltpu.SMEM)] + [whole()] * len(pieces),
        out_specs=whole(pl.ANY),
        scratch_shapes=[pltpu.SemaphoreType.DMA((len(pieces),))],
        compiler_params=pltpu.CompilerParams(vmem_limit_bytes=VMEM_LIMIT),
        name="fill",
    )(where, *pieces)


TILE_COLS = 4
AXES = ("y", "zh", "x", "core", "zl")
SIZES = (4, 2, 4, 2, 4)
TILE_AXES = AXES[:4]


def mirrored(tile, group):
    z_hi = tile // 8 % 2
    return group if z_hi == 0 else GROUPS - 1 - group


def across_columns(block, step):
    route = [(t, t + step) for t in range(64) if 0 <= t % TILE_COLS + step < TILE_COLS]
    return lax.ppermute(block, TILE_AXES, route)


def across_rows(block, step):
    route = []
    for t in range(64):
        u = t + step * TILE_COLS
        if 0 <= u < 64:
            for k in range(GROUPS):
                route.append((t * GROUPS + mirrored(t, k), u * GROUPS + mirrored(u, k)))
    return lax.ppermute(block, AXES, route)


def among(block, axis, distance):
    n = lax.axis_size(axis)
    return lax.ppermute(block, axis, [(i, i ^ distance) for i in range(n)])


def exchange(block, distance, stage):
    route = []
    for y, zh, x, core, zl in np.ndindex(*SIZES):
        to = (y, zh, x ^ distance, core, zl) if core == stage else (y ^ distance, zh, x, core, zl)
        route.append((int(np.ravel_multi_index((y, zh, x, core, zl), SIZES)), int(np.ravel_multi_index(to, SIZES))))
    return lax.ppermute(block, AXES, route)


def exchanged(pieces, stage):
    return [exchange(pieces[d], d, stage) for d in (1, 2, 3)]


def tied(*groups):
    return lax.optimization_barrier(tuple(groups))


def by_place(pieces, me):
    one, two = me % 2 == 1, me // 2 == 1
    pairs = [(jnp.where(one, b, a), jnp.where(one, a, b)) for a, b in (pieces[:2], pieces[2:])]
    low = [jnp.where(two, q, p) for p, q in zip(*pairs)]
    high = [jnp.where(two, p, q) for p, q in zip(*pairs)]
    return jnp.concatenate(low + high)


def total_of(pieces):
    return (pieces[0] + pieces[1]) + (pieces[2] + pieces[3])


def by_parity(amplitude):
    pattern = amplitude.shape[0]
    order = np.concatenate([np.arange(0, pattern, 2), np.arange(1, pattern, 2)])
    table = jnp.asarray(np.eye(pattern, dtype=np.float32)[order])
    exact = lax.Precision.HIGHEST
    return jnp.dot(jnp.dot(table, amplitude, precision=exact), table.T, precision=exact)


def shards(object_tiles, probe, offsets, amplitude):
    own_tile = object_tiles[0]
    pattern = probe.shape[-1]
    tile_side = own_tile.shape[-1]
    place = offsets[0, 0]
    x, y, core, z_hi, z_lo = (lax.axis_index(axis) for axis in ("x", "y", "core", "zh", "zl"))
    row_class = jnp.where(z_hi == 0, z_lo, GROUPS - 1 - z_lo)
    turn, next_turn = jnp.where(core == 0, x, y), jnp.where(core == 0, y, x)
    where = jnp.stack([place[0], core, row_class, turn, next_turn]).astype(jnp.int32)
    own_class = where[2:3]
    tables = [jnp.asarray(table) for table in dft_tables(pattern)]

    blocks = own_tile.reshape(2, -1, GROUPS, ROW_BLOCK, tile_side)
    class_rows = lax.dynamic_index_in_dim(blocks, row_class, 2, keepdims=False).reshape(2, -1, tile_side)
    low = across_rows(class_rows[:, : pattern // GROUPS], -1)
    right = across_columns(class_rows[:, :, :pattern], -1)
    right, place_later = tied(right, place)
    spots = [place] + [among(place_later, "zl", d) for d in (1, 2, 3)]
    target = by_parity(amplitude[0, 0])
    low, spots, target = tied(low, spots, target)
    corner = across_columns(low[:, :, :pattern], -1)
    rows = list(cut_call(own_class, spots, blocks, right, low, corner))
    rows = rows[:1] + [among(rows[d], "zl", d) for d in (1, 2, 3)]

    sent, corrected, patch, term = first_call(where, rows, probe, target, tables)
    arrived = among(sent, "core", 1)
    kept, *rows = second_call(where, corrected, patch, term, probe, tables)

    pieces = [(kept[d] + arrived[d]).reshape(-1, pattern) for d in range(4)]
    pieces, rows = tied(pieces, rows)
    pieces = pieces[:1] + exchanged(pieces, 0)
    rows = rows[:1] + [among(rows[d], "zl", d) for d in (1, 2, 3)]
    mine = total_of(pieces).reshape(4, -1, pattern)
    body, margin = place_call(own_class, spots, rows, tile_side)
    inside = tile_side // GROUPS

    pieces = [lax.dynamic_index_in_dim(mine, next_turn ^ d, 0, keepdims=False) for d in range(4)]
    pieces, margin = tied(pieces, margin)
    body = body.at[:, :, :pattern].add(across_columns(margin, 1))
    pieces = pieces[:1] + exchanged(pieces, 1)
    mine = total_of(pieces).reshape(8, -1, pattern)

    mine, lower = tied(mine, body[:, inside:])
    from_above = across_rows(lower, 1)
    spread = lax.all_to_all(mine, ("zh", "zl"), 0, 0, tiled=True)
    mine = jnp.sum(spread, axis=0) * (1.0 / math.sqrt(mesh_size()))
    body = body[:, :inside].at[:, : pattern // GROUPS].add(from_above)

    spread, body = tied(jnp.broadcast_to(mine[None], (8,) + mine.shape), body)
    second = among(body, "zl", 2)
    mine = lax.all_to_all(spread, ("zh", "zl"), 0, 0, tiled=True).reshape(-1, pattern)
    mine, body, second = tied(mine, body, second)
    first = among(body, "zl", 1)
    mine = by_place([mine] + [exchange(mine, d, 1) for d in (1, 2, 3)], next_turn)
    mine, body, first = tied(mine, body, first)
    third = among(body, "zl", 3)
    pieces = exchanged([mine] * 4, 0)
    other = [among(mine, "core", 1)]
    pieces, third = tied(pieces, third)
    other = other + [among(piece, "core", 1) for piece in pieces]
    return (join_call(own_class, [body, first, second, third]), fill_call(where, [mine, *pieces, *other], probe.shape))


def mesh_size():
    return math.prod(SIZES)


def solution(mesh):
    fine = Mesh(mesh.devices.reshape(SIZES), AXES)
    placed = (
        P(TILE_AXES, None, None, None),
        P(),
        P(TILE_AXES, "zl", None),
        P(TILE_AXES, "zl", None, None),
    )
    return jax.shard_map(
        shards,
        mesh=fine,
        in_specs=placed,
        out_specs=(P(TILE_AXES, None, None, None), P()),
        check_vma=False,
    )
```

```python
import functools
import math

import jax
import jax.numpy as jnp
import ml_dtypes
import numpy as np
from jax import lax
from jax.experimental import pallas as pl
from jax.experimental.pallas import tpu as pltpu
from jax.sharding import Mesh, PartitionSpec as P

GROUPS = 4
ROW_BLOCK = 8
BF16 = jnp.bfloat16
F32 = jnp.float32
VMEM_LIMIT = 48 * 1024 * 1024


def split_table(table):
    high = table.astype(ml_dtypes.bfloat16)
    low = (table - high.astype(np.float64)).astype(ml_dtypes.bfloat16)
    return high, low


def dft_tables(pattern):
    half = pattern // 2
    angles = 2.0 * np.pi / half * (np.outer(np.arange(half), np.arange(half)) % half)
    cosine, sine = np.cos(angles) / math.sqrt(pattern), np.sin(angles) / math.sqrt(pattern)
    table = np.block([[cosine, -sine], [sine, cosine]])
    high, low = split_table(table)
    down = np.concatenate([high, high, low], axis=0)
    across = np.concatenate([high, high, low], axis=1)
    turned = [np.ascontiguousarray(part.T) for part in (high, low)]
    down_t = np.concatenate([turned[0], turned[0], turned[1]], axis=0)
    across_t = np.concatenate([turned[0], turned[0], turned[1]], axis=1)
    twist = 2.0 * np.pi / pattern * np.arange(half)
    lanes = np.stack([np.cos(twist), -np.sin(twist)])[:, None, :].astype(np.float32)
    rows = np.ascontiguousarray(
        np.broadcast_to(np.stack([np.cos(twist), -np.sin(twist)])[:, :, None], (2, half, half))
    ).astype(np.float32)
    return down, across, down_t, across_t, lanes, rows


def parts(x):
    high = x.astype(BF16)
    return high, (x - high.astype(F32)).astype(BF16)


def times(x, table):
    high, low = parts(x)
    return jnp.dot(jnp.concatenate([high, low, high], axis=1), table, preferred_element_type=F32)


def under(table, x):
    high, low = parts(x)
    return jnp.dot(table, jnp.concatenate([high, low, high], axis=0), preferred_element_type=F32)


def forward(re, im, down, across_t, lanes, rows):
    h = re.shape[0] // 2
    wr, wi = lanes
    a, b, c, d = re[:, :h], re[:, h:], im[:, :h], im[:, h:]
    p, q = a - b, c - d
    even = times(jnp.concatenate([a + b, c + d], axis=1), down)
    odd = times(jnp.concatenate([p * wr - q * wi, p * wi + q * wr], axis=1), down)
    re = jnp.concatenate([even[:, :h], odd[:, :h]], axis=1)
    im = jnp.concatenate([even[:, h:], odd[:, h:]], axis=1)
    wr, wi = rows
    a, b, c, d = re[:h], re[h:], im[:h], im[h:]
    p, q = a - b, c - d
    even = under(across_t, jnp.concatenate([a + b, c + d], axis=0))
    odd = under(across_t, jnp.concatenate([p * wr - q * wi, p * wi + q * wr], axis=0))
    return jnp.concatenate([even[:h], odd[:h]], axis=0), jnp.concatenate([even[h:], odd[h:]], axis=0)


def backward(re, im, down_t, across, lanes, rows):
    h = re.shape[0] // 2
    wr, wi = rows
    even = under(across, jnp.concatenate([re[:h], im[:h]], axis=0))
    odd = under(across, jnp.concatenate([re[h:], im[h:]], axis=0))
    p, q = odd[:h], odd[h:]
    p, q = p * wr + q * wi, q * wr - p * wi
    re = jnp.concatenate([even[:h] + p, even[:h] - p], axis=0)
    im = jnp.concatenate([even[h:] + q, even[h:] - q], axis=0)
    wr, wi = lanes
    even = times(jnp.concatenate([re[:, :h], im[:, :h]], axis=1), down_t)
    odd = times(jnp.concatenate([re[:, h:], im[:, h:]], axis=1), down_t)
    p, q = odd[:, :h], odd[:, h:]
    p, q = p * wr + q * wi, q * wr - p * wi
    re = jnp.concatenate([even[:, :h] + p, even[:, :h] - p], axis=1)
    im = jnp.concatenate([even[:, h:] + q, even[:, h:] - q], axis=1)
    return re, im


def twiddles(lanes_ref, rows_ref):
    rows = [jnp.concatenate([rows_ref[i], rows_ref[i]], axis=1) for i in range(2)]
    return (lanes_ref[0], lanes_ref[1]), rows


def gradients(re, im, m, i, patch_ref, probe_ref, term, grad_ref, tables):
    re, im = backward(re, im, *tables)
    grad_ref[i, 0] = patch_ref[0] * re + patch_ref[1] * im
    grad_ref[i, 1] = patch_ref[0] * im - patch_ref[1] * re
    probe_re, probe_im = probe_ref[m, 0].astype(F32), probe_ref[m, 1].astype(F32)
    term[0] += probe_re * re + probe_im * im
    term[1] += probe_re * im - probe_im * re


def first_kernel(
    where_ref, rows0, rows1, rows2, rows3, probe_ref, amplitude_ref, down, across, down_t, across_t, lanes_ref, rows_ref,
    sent_ref, corrected_ref, patch_ref, term_ref, frame, far, total,
):
    pattern = amplitude_ref.shape[0]
    modes = probe_ref.shape[0]
    half = modes // 2
    row_at, core, other_turn = where_ref[0], where_ref[1], where_ref[4]
    turn = where_ref[3]
    block, shift = row_at // ROW_BLOCK, row_at % ROW_BLOCK
    count = frame.shape[1]
    for d, rows in enumerate((rows0, rows1, rows2, rows3)):
        first = ((where_ref[2] ^ d) + GROUPS - block % GROUPS) % GROUPS
        for i in range(count // GROUPS):
            frame[:, first + GROUPS * i] = rows[:, i]
    height = pattern + ROW_BLOCK
    for channel in range(2):
        window = frame[channel, : count - 3].reshape(height, pattern)
        patch_ref[channel] = pltpu.roll(window, (height - shift) % height, 0)[:pattern]
    lanes, rows = twiddles(lanes_ref, rows_ref)
    total[...] = jnp.full_like(total, 0.01)

    def outward(m, carry):
        probe_re, probe_im = probe_ref[m, 0].astype(F32), probe_ref[m, 1].astype(F32)
        re = probe_re * patch_ref[0] - probe_im * patch_ref[1]
        im = probe_re * patch_ref[1] + probe_im * patch_ref[0]
        re, im = forward(re, im, down[...], across_t[...], lanes, rows)
        far[m, 0] = re
        far[m, 1] = im
        total[...] += re * re + im * im
        return carry

    lax.fori_loop(0, modes, outward, 0, unroll=UNROLL)
    total[...] = 1.0 - amplitude_ref[...] * lax.rsqrt(total[...])
    term_ref[...] = jnp.zeros_like(term_ref)
    tables = (down_t[...], across[...], lanes, rows)

    def homeward(i, carry):
        m = (1 - core) * half + (other_turn ^ i)
        kept = core * half + (turn ^ i)
        corrected_ref[i, 0] = far[kept, 0] * total[...]
        corrected_ref[i, 1] = far[kept, 1] * total[...]
        gradients(far[m, 0] * total[...], far[m, 1] * total[...], m, i, patch_ref, probe_ref, term_ref, sent_ref, tables)
        return carry

    lax.fori_loop(0, half, homeward, 0, unroll=UNROLL)


def second_kernel(
    where_ref, corrected_ref, patch_ref, term_ref, probe_ref, across, down_t, lanes_ref, rows_ref,
    kept_ref, rows0, rows1, rows2, rows3, term, frame,
):
    pattern = patch_ref.shape[1]
    half = corrected_ref.shape[0]
    row_at, core, row_class, turn = where_ref[0], where_ref[1], where_ref[2], where_ref[3]
    lanes, rows = twiddles(lanes_ref, rows_ref)
    tables = (down_t[...], across[...], lanes, rows)
    term[...] = term_ref[...]

    def homeward(i, carry):
        gradients(
            corrected_ref[i, 0],
            corrected_ref[i, 1],
            core * half + (turn ^ i),
            i,
            patch_ref,
            probe_ref,
            term,
            kept_ref,
            tables,
        )
        return carry

    lax.fori_loop(0, half, homeward, 0, unroll=UNROLL)
    block = row_at // ROW_BLOCK
    shift = row_at % ROW_BLOCK
    count = frame.shape[1]
    for channel in range(2):
        padded = jnp.concatenate([term[channel], jnp.zeros((ROW_BLOCK, pattern), F32)], axis=0)
        frame[channel, : count - 3] = pltpu.roll(padded, shift, 0).reshape(count - 3, ROW_BLOCK, pattern)
        frame[channel, count - 3 :] = jnp.zeros((3, ROW_BLOCK, pattern), F32)
    for d, out in enumerate((rows0, rows1, rows2, rows3)):
        first = ((row_class ^ d) + GROUPS - block % GROUPS) % GROUPS
        for i in range(count // GROUPS):
            out[:, i] = frame[:, first + GROUPS * i]


def whole(space=pltpu.VMEM):
    return pl.BlockSpec(memory_space=space)


UNROLL = 4


def first_call(where, pieces, probe, amplitude, tables):
    modes, _, pattern, _ = probe.shape
    half = (modes // 2, 2, pattern, pattern)
    shapes = [half, half, (2, pattern, pattern), (2, pattern, pattern)]
    return pl.pallas_call(
        first_kernel,
        out_shape=[jax.ShapeDtypeStruct(s, F32) for s in shapes],
        in_specs=[whole(pltpu.SMEM)] + [whole()] * 12,
        out_specs=[whole()] * 4,
        scratch_shapes=[
            pltpu.VMEM((2, pattern // ROW_BLOCK + GROUPS, ROW_BLOCK, pattern), F32),
            pltpu.VMEM((modes, 2, pattern, pattern), F32),
            pltpu.VMEM((pattern, pattern), F32),
        ],
        compiler_params=pltpu.CompilerParams(vmem_limit_bytes=VMEM_LIMIT),
        name="outward",
    )(where, *pieces, probe, amplitude, *tables)


def second_call(where, corrected, patch, term, probe, tables):
    down, across, down_t, across_t, lanes, rows = tables
    pattern = patch.shape[1]
    blocks = pattern // ROW_BLOCK + GROUPS
    piece = (2, blocks // GROUPS, ROW_BLOCK, pattern)
    shapes = [corrected.shape] + [piece] * GROUPS
    return pl.pallas_call(
        second_kernel,
        out_shape=[jax.ShapeDtypeStruct(s, F32) for s in shapes],
        in_specs=[whole(pltpu.SMEM)] + [whole()] * 8,
        out_specs=[whole()] * 5,
        scratch_shapes=[
            pltpu.VMEM((2, pattern, pattern), F32),
            pltpu.VMEM((2, blocks, ROW_BLOCK, pattern), F32),
        ],
        compiler_params=pltpu.CompilerParams(vmem_limit_bytes=VMEM_LIMIT),
        name="homeward",
    )(where, corrected, patch, term, probe, across, down_t, lanes, rows)


def class_start(spot, row_class):
    block = spot[0] // ROW_BLOCK
    start = (block + (row_class + GROUPS - block % GROUPS) % GROUPS) // GROUPS
    return pl.multiple_of(start * ROW_BLOCK, ROW_BLOCK)


def cut_kernel(
    class_ref, spot0, spot1, spot2, spot3, tile_ref, right_ref, low_ref, corner_ref, rows0, rows1, rows2, rows3, owned
):
    row_class = class_ref[0]
    _, blocks, _, _, side = tile_ref.shape
    inside = blocks * ROW_BLOCK
    _, outside, _ = low_ref.shape
    for i in range(blocks):
        owned[:, ROW_BLOCK * i : ROW_BLOCK * (i + 1), :side] = tile_ref[:, i, row_class]
    owned[:, :inside, side:] = right_ref[...]
    owned[:, inside : inside + outside, :side] = low_ref[...]
    owned[:, inside : inside + outside, side:] = corner_ref[...]
    owned[:, inside + outside :] = jnp.zeros((2, ROW_BLOCK, owned.shape[2]), F32)
    for spot, rows in ((spot0, rows0), (spot1, rows1), (spot2, rows2), (spot3, rows3)):
        _, count, _, width = rows.shape
        col_at = spot[1]
        down = pl.ds(class_start(spot, row_class), count * ROW_BLOCK)
        across = pl.ds(pl.multiple_of(col_at // 128 * 128, 128), width + 128)
        for channel in range(2):
            wide = pltpu.roll(owned[channel, down, across], (width + 128 - col_at % 128) % (width + 128), 1)
            rows[channel] = wide[:, :width].reshape(count, ROW_BLOCK, width)


def cut_call(row_class, spots, tile, right, low, corner):
    _, blocks, _, _, side = tile.shape
    width = right.shape[2]
    piece = (2, (width // ROW_BLOCK + GROUPS) // GROUPS, ROW_BLOCK, width)
    return pl.pallas_call(
        cut_kernel,
        out_shape=[jax.ShapeDtypeStruct(piece, F32)] * GROUPS,
        in_specs=[whole(pltpu.SMEM)] * 5 + [whole()] * 4,
        out_specs=[whole()] * GROUPS,
        scratch_shapes=[pltpu.VMEM((2, (side + width) // GROUPS + ROW_BLOCK, side + width), F32)],
        compiler_params=pltpu.CompilerParams(vmem_limit_bytes=VMEM_LIMIT),
        name="cut",
    )(row_class, *spots, tile, right, low, corner)


def place_kernel(class_ref, spot0, spot1, spot2, spot3, rows0, rows1, rows2, rows3, body_ref, margin_ref, owned):
    row_class = class_ref[0]
    owned[...] = jnp.zeros_like(owned)
    for spot, rows in ((spot0, rows0), (spot1, rows1), (spot2, rows2), (spot3, rows3)):
        _, count, _, width = rows.shape
        col_at = spot[1]
        down = pl.ds(class_start(spot, row_class), count * ROW_BLOCK)
        across = pl.ds(pl.multiple_of(col_at // 128 * 128, 128), width + 128)
        for channel in range(2):
            block_rows = rows[channel].reshape(count * ROW_BLOCK, width)
            wide = jnp.concatenate([block_rows, jnp.zeros((count * ROW_BLOCK, 128), F32)], axis=1)
            owned[channel, down, across] += pltpu.roll(wide, col_at % 128, 1)
    height, side = body_ref.shape[1:]
    body_ref[...] = owned[:, :height, :side]
    margin_ref[...] = owned[:, :height, side:]


def place_call(row_class, spots, pieces, side):
    _, count, _, width = pieces[0].shape
    height = (side + width) // GROUPS
    return pl.pallas_call(
        place_kernel,
        out_shape=[jax.ShapeDtypeStruct((2, height, w), F32) for w in (side, width)],
        in_specs=[whole(pltpu.SMEM)] * 5 + [whole()] * 4,
        out_specs=[whole()] * 2,
        scratch_shapes=[pltpu.VMEM((2, height + ROW_BLOCK, side + width), F32)],
        compiler_params=pltpu.CompilerParams(vmem_limit_bytes=VMEM_LIMIT),
        name="place",
    )(row_class, *spots, *pieces)


def join_kernel(class_ref, rows0, rows1, rows2, rows3, out_ref):
    for d, rows in enumerate((rows0, rows1, rows2, rows3)):
        place = class_ref[0] ^ d
        for i in range(out_ref.shape[1]):
            out_ref[:, i, place] = rows[:, ROW_BLOCK * i : ROW_BLOCK * (i + 1)]


def join_call(row_class, pieces):
    _, height, side = pieces[0].shape
    out = pl.pallas_call(
        join_kernel,
        out_shape=jax.ShapeDtypeStruct((2, height // ROW_BLOCK, GROUPS, ROW_BLOCK, side), F32),
        in_specs=[whole(pltpu.SMEM)] + [whole()] * 4,
        out_specs=whole(),
        compiler_params=pltpu.CompilerParams(vmem_limit_bytes=VMEM_LIMIT),
        name="join",
    )(row_class, *pieces)
    return out.reshape(1, 2, height * GROUPS, side)


def fill_kernel(slots, count, where_ref, *refs):
    pieces, out_ref, sems = refs[:count], refs[-2], refs[-1]
    core, turns = where_ref[1], (where_ref[3], where_ref[4])
    half = out_ref.shape[0] // 2
    copies = []
    for piece, homes in zip(pieces, slots):
        for i, (side, d, part) in enumerate(homes):
            target = out_ref.at[half * (core ^ side) + (turns[side] ^ d), part]
            copies.append(pltpu.make_async_copy(piece.at[i], target, sems.at[len(copies)]))
    for copy in copies:
        copy.start()
    for copy in copies:
        copy.wait()


def fill_call(where, pieces, slots, shape, base=None):
    pieces = [piece.reshape(-1, *shape[2:]) for piece in pieces]
    given = [] if base is None else [base]
    return pl.pallas_call(
        functools.partial(fill_kernel, slots, len(pieces)),
        out_shape=jax.ShapeDtypeStruct(shape, F32),
        in_specs=[whole(pltpu.SMEM)] + [whole()] * len(pieces) + [whole(pl.ANY)] * len(given),
        out_specs=whole(pl.ANY),
        scratch_shapes=[pltpu.SemaphoreType.DMA((sum(len(homes) for homes in slots),))],
        input_output_aliases={1 + len(pieces): 0} if given else {},
        compiler_params=pltpu.CompilerParams(vmem_limit_bytes=VMEM_LIMIT),
        name="fill",
    )(where, *pieces, *given)


TILE_COLS = 4
AXES = ("y", "zh", "x", "core", "zl")
SIZES = (4, 2, 4, 2, 4)
TILE_AXES = AXES[:4]


def mirrored(tile, group):
    z_hi = tile // 8 % 2
    return group if z_hi == 0 else GROUPS - 1 - group


def across_columns(block, step):
    route = [(t, t + step) for t in range(64) if 0 <= t % TILE_COLS + step < TILE_COLS]
    return lax.ppermute(block, TILE_AXES, route)


def across_rows(block, step, columns=0):
    route = []
    for t in range(64):
        u = t + step * TILE_COLS + columns
        if 0 <= u < 64 and 0 <= t % TILE_COLS + columns < TILE_COLS:
            for k in range(GROUPS):
                route.append((t * GROUPS + mirrored(t, k), u * GROUPS + mirrored(u, k)))
    return lax.ppermute(block, AXES, route)


def among(block, axis, distance):
    n = lax.axis_size(axis)
    return lax.ppermute(block, axis, [(i, i ^ distance) for i in range(n)])


def exchange(block, distance, stage):
    route = []
    for y, zh, x, core, zl in np.ndindex(*SIZES):
        to = (y, zh, x ^ distance, core, zl) if core == stage else (y ^ distance, zh, x, core, zl)
        route.append((int(np.ravel_multi_index((y, zh, x, core, zl), SIZES)), int(np.ravel_multi_index(to, SIZES))))
    return lax.ppermute(block, AXES, route)


def opposite(block):
    route = []
    for y, zh, x, core, zl in np.ndindex(*SIZES):
        to = (y, 1 - zh, x, core, GROUPS - 1 - zl)
        route.append((int(np.ravel_multi_index((y, zh, x, core, zl), SIZES)), int(np.ravel_multi_index(to, SIZES))))
    return lax.ppermute(block, AXES, route)


def exchanged(pieces, stage):
    return [exchange(pieces[d], d, stage) for d in (1, 2, 3)]


def swapped(blocks):
    ranks = np.arange(math.prod(SIZES)).reshape(SIZES)
    groups = [ranks[y, zh, x, core, :: 1 - 2 * zh].tolist() for y, zh, x, core in np.ndindex(*SIZES[:4])]
    return lax.all_to_all(blocks, AXES, 0, 0, axis_index_groups=groups, tiled=True)


def tied(*groups):
    return lax.optimization_barrier(tuple(groups))


def by_place(pieces, me):
    one, two = me % 2 == 1, me // 2 == 1
    pairs = [(jnp.where(one, b, a), jnp.where(one, a, b)) for a, b in (pieces[:2], pieces[2:])]
    low = [jnp.where(two, q, p) for p, q in zip(*pairs)]
    high = [jnp.where(two, p, q) for p, q in zip(*pairs)]
    return jnp.concatenate(low + high)


def total_of(pieces):
    return (pieces[0] + pieces[1]) + (pieces[2] + pieces[3])


def by_parity(amplitude):
    pattern = amplitude.shape[0]
    order = np.concatenate([np.arange(0, pattern, 2), np.arange(1, pattern, 2)])
    table = jnp.asarray(np.eye(pattern, dtype=np.float32)[order])
    exact = lax.Precision.HIGHEST
    return jnp.dot(jnp.dot(table, amplitude, precision=exact), table.T, precision=exact)


def shards(object_tiles, probe, offsets, amplitude):
    own_tile = object_tiles[0]
    pattern = probe.shape[-1]
    tile_side = own_tile.shape[-1]
    place = offsets[0, 0]
    x, y, core, z_hi, z_lo = (lax.axis_index(axis) for axis in ("x", "y", "core", "zh", "zl"))
    row_class = jnp.where(z_hi == 0, z_lo, GROUPS - 1 - z_lo)
    turn, next_turn = jnp.where(core == 0, x, y), jnp.where(core == 0, y, x)
    where = jnp.stack([place[0], core, row_class, turn, next_turn]).astype(jnp.int32)
    own_class = where[2:3]
    tables = [jnp.asarray(table) for table in dft_tables(pattern)]

    blocks = own_tile.reshape(2, -1, GROUPS, ROW_BLOCK, tile_side)
    class_rows = lax.dynamic_index_in_dim(blocks, row_class, 2, keepdims=False).reshape(2, -1, tile_side)
    outside = pattern // GROUPS
    low = across_rows(class_rows[:, :outside], -1)
    corner = across_rows(class_rows[:, :outside, :pattern], -1, -1)
    right = across_columns(class_rows[:, :, :pattern], -1)
    right, place_later = tied(right, place)
    spots = [place] + [among(place_later, "zl", d) for d in (1, 2, 3)]
    target = by_parity(amplitude[0, 0])
    rows = list(cut_call(own_class, spots, blocks, right, low, corner))
    rows = rows[:1] + [among(rows[d], "zl", d) for d in (1, 2, 3)]

    sent, corrected, patch, term = first_call(where, rows, probe, target, tables)
    arrived = among(sent, "core", 1)
    kept, *rows = second_call(where, corrected, patch, term, probe, tables)

    pieces = [(kept[d] + arrived[d]).reshape(-1, pattern) for d in range(4)]
    pieces, rows = tied(pieces, rows)
    pieces = pieces[:1] + exchanged(pieces, 0)
    rows = rows[:1] + [among(rows[d], "zl", d) for d in (1, 2, 3)]
    mine = total_of(pieces).reshape(4, -1, pattern)
    body, margin = place_call(own_class, spots, rows, tile_side)
    inside = tile_side // GROUPS

    pieces = [lax.dynamic_index_in_dim(mine, next_turn ^ d, 0, keepdims=False) for d in range(4)]
    pieces, margin = tied(pieces, margin)
    body = body.at[:, :, :pattern].add(across_columns(margin, 1))
    pieces = pieces[:1] + exchanged(pieces, 1)
    mine = total_of(pieces).reshape(8, -1, pattern)

    mine = total_of(pieces).reshape(GROUPS, -1, pattern)
    mine, lower = tied(mine, body[:, inside:])
    from_above = across_rows(lower, 1)
    mine = jnp.sum(swapped(mine), axis=0)
    mine = (mine + opposite(mine)) * (1.0 / math.sqrt(mesh_size()))
    body = body[:, :inside].at[:, :outside].add(from_above)

    mine, body = tied(mine, body)
    second = among(body[0], "zl", 2)
    near = [among(mine, "zl", d) for d in (1, 2, 3)]
    near, second, body = tied(near, second, body)
    later = among(body[1], "zl", 2)
    mine = by_place([mine, *near], row_class)
    near = [exchange(mine, d, 1) for d in (1, 2, 3)]
    near, later = tied(near, later)
    second = jnp.stack([second, later])
    mine = by_place([mine, *near], next_turn)
    mine, pair = tied(mine, jnp.stack([body, second]))
    pair = among(pair, "zl", 1)
    pieces = [mine] + exchanged([mine] * 4, 0)
    homes = [[((side, d, 0), (side, d, 1)) for side in range(2)] for d in range(4)]
    *pieces[2:], pair = tied(*pieces[2:], pair)
    other = [among(piece, "core", 1) for piece in pieces]
    done = [pieces[0], other[0], pieces[1], other[1], pieces[2], pieces[3]]
    grad = fill_call(where, done, homes[0] + homes[1] + homes[2][:1] + homes[3][:1], probe.shape)
    grad = fill_call(where, other[2:], homes[2][1:] + homes[3][1:], probe.shape, grad)
    return (join_call(own_class, [body, pair[0], second, pair[1]]), grad)


def mesh_size():
    return math.prod(SIZES)


def solution(mesh):
    fine = Mesh(mesh.devices.reshape(SIZES), AXES)
    placed = (
        P(TILE_AXES, None, None, None),
        P(),
        P(TILE_AXES, "zl", None),
        P(TILE_AXES, "zl", None, None),
    )
    return jax.shard_map(
        shards,
        mesh=fine,
        in_specs=placed,
        out_specs=(P(TILE_AXES, None, None, None), P()),
        check_vma=False,
    )
```

```python
import functools
import math

import jax
import jax.numpy as jnp
import ml_dtypes
import numpy as np
from jax import lax
from jax.experimental import pallas as pl
from jax.experimental.pallas import tpu as pltpu
from jax.sharding import Mesh, PartitionSpec as P

GROUPS = 4
ROW_BLOCK = 8
BF16 = jnp.bfloat16
F32 = jnp.float32
VMEM_LIMIT = 48 * 1024 * 1024


def split_table(table):
    high = table.astype(ml_dtypes.bfloat16)
    low = (table - high.astype(np.float64)).astype(ml_dtypes.bfloat16)
    return high, low


def dft_tables(pattern):
    half = pattern // 2
    angles = 2.0 * np.pi / half * (np.outer(np.arange(half), np.arange(half)) % half)
    cosine, sine = np.cos(angles) / math.sqrt(pattern), np.sin(angles) / math.sqrt(pattern)
    table = np.block([[cosine, -sine], [sine, cosine]])
    high, low = split_table(table)
    down = np.concatenate([high, high, low], axis=0)
    across = np.concatenate([high, high, low], axis=1)
    turned = [np.ascontiguousarray(part.T) for part in (high, low)]
    down_t = np.concatenate([turned[0], turned[0], turned[1]], axis=0)
    across_t = np.concatenate([turned[0], turned[0], turned[1]], axis=1)
    twist = 2.0 * np.pi / pattern * np.arange(half)
    lanes = np.stack([np.cos(twist), -np.sin(twist)])[:, None, :].astype(np.float32)
    rows = np.ascontiguousarray(
        np.broadcast_to(np.stack([np.cos(twist), -np.sin(twist)])[:, :, None], (2, half, half))
    ).astype(np.float32)
    return down, across, down_t, across_t, lanes, rows


def parts(x):
    high = x.astype(BF16)
    return high, (x - high.astype(F32)).astype(BF16)


def times(x, table):
    high, low = parts(x)
    return jnp.dot(jnp.concatenate([high, low, high], axis=1), table, preferred_element_type=F32)


def under(table, x):
    high, low = parts(x)
    return jnp.dot(table, jnp.concatenate([high, low, high], axis=0), preferred_element_type=F32)


def forward(re, im, down, across_t, lanes, rows):
    h = re.shape[0] // 2
    wr, wi = lanes
    a, b, c, d = re[:, :h], re[:, h:], im[:, :h], im[:, h:]
    p, q = a - b, c - d
    even = times(jnp.concatenate([a + b, c + d], axis=1), down)
    odd = times(jnp.concatenate([p * wr - q * wi, p * wi + q * wr], axis=1), down)
    re = jnp.concatenate([even[:, :h], odd[:, :h]], axis=1)
    im = jnp.concatenate([even[:, h:], odd[:, h:]], axis=1)
    wr, wi = rows
    a, b, c, d = re[:h], re[h:], im[:h], im[h:]
    p, q = a - b, c - d
    even = under(across_t, jnp.concatenate([a + b, c + d], axis=0))
    odd = under(across_t, jnp.concatenate([p * wr - q * wi, p * wi + q * wr], axis=0))
    return jnp.concatenate([even[:h], odd[:h]], axis=0), jnp.concatenate([even[h:], odd[h:]], axis=0)


def backward(re, im, down_t, across, lanes, rows):
    h = re.shape[0] // 2
    wr, wi = rows
    even = under(across, jnp.concatenate([re[:h], im[:h]], axis=0))
    odd = under(across, jnp.concatenate([re[h:], im[h:]], axis=0))
    p, q = odd[:h], odd[h:]
    p, q = p * wr + q * wi, q * wr - p * wi
    re = jnp.concatenate([even[:h] + p, even[:h] - p], axis=0)
    im = jnp.concatenate([even[h:] + q, even[h:] - q], axis=0)
    wr, wi = lanes
    even = times(jnp.concatenate([re[:, :h], im[:, :h]], axis=1), down_t)
    odd = times(jnp.concatenate([re[:, h:], im[:, h:]], axis=1), down_t)
    p, q = odd[:, :h], odd[:, h:]
    p, q = p * wr + q * wi, q * wr - p * wi
    re = jnp.concatenate([even[:, :h] + p, even[:, :h] - p], axis=1)
    im = jnp.concatenate([even[:, h:] + q, even[:, h:] - q], axis=1)
    return re, im


def twiddles(lanes_ref, rows_ref):
    rows = [jnp.concatenate([rows_ref[i], rows_ref[i]], axis=1) for i in range(2)]
    return (lanes_ref[0], lanes_ref[1]), rows


def gradients(re, im, m, i, patch_ref, probe_ref, term, grad_ref, tables):
    re, im = backward(re, im, *tables)
    grad_ref[i, 0] = patch_ref[0] * re + patch_ref[1] * im
    grad_ref[i, 1] = patch_ref[0] * im - patch_ref[1] * re
    probe_re, probe_im = probe_ref[m, 0].astype(F32), probe_ref[m, 1].astype(F32)
    term[0] += probe_re * re + probe_im * im
    term[1] += probe_re * im - probe_im * re


def first_kernel(
    where_ref, rows0, rows1, rows2, rows3, probe_ref, amplitude_ref, down, across, down_t, across_t, lanes_ref, rows_ref,
    sent_ref, corrected_ref, patch_ref, term_ref, frame, far, total,
):
    pattern = amplitude_ref.shape[0]
    modes = probe_ref.shape[0]
    half = modes // 2
    row_at, core, other_turn = where_ref[0], where_ref[1], where_ref[4]
    turn = where_ref[3]
    block, shift = row_at // ROW_BLOCK, row_at % ROW_BLOCK
    count = frame.shape[1]
    for d, rows in enumerate((rows0, rows1, rows2, rows3)):
        first = ((where_ref[2] ^ d) + GROUPS - block % GROUPS) % GROUPS
        for i in range(count // GROUPS):
            frame[:, first + GROUPS * i] = rows[:, i]
    height = pattern + ROW_BLOCK
    for channel in range(2):
        window = frame[channel, : count - 3].reshape(height, pattern)
        patch_ref[channel] = pltpu.roll(window, (height - shift) % height, 0)[:pattern]
    lanes, rows = twiddles(lanes_ref, rows_ref)
    total[...] = jnp.full_like(total, 0.01)

    def outward(m, carry):
        probe_re, probe_im = probe_ref[m, 0].astype(F32), probe_ref[m, 1].astype(F32)
        re = probe_re * patch_ref[0] - probe_im * patch_ref[1]
        im = probe_re * patch_ref[1] + probe_im * patch_ref[0]
        re, im = forward(re, im, down[...], across_t[...], lanes, rows)
        far[m, 0] = re
        far[m, 1] = im
        total[...] += re * re + im * im
        return carry

    lax.fori_loop(0, modes, outward, 0, unroll=2 * UNROLL)
    total[...] = 1.0 - amplitude_ref[...] * lax.rsqrt(total[...])
    term_ref[...] = jnp.zeros_like(term_ref)
    tables = (down_t[...], across[...], lanes, rows)

    def homeward(i, carry):
        m = (1 - core) * half + (other_turn ^ i)
        kept = core * half + (turn ^ i)
        corrected_ref[i, 0] = far[kept, 0] * total[...]
        corrected_ref[i, 1] = far[kept, 1] * total[...]
        gradients(far[m, 0] * total[...], far[m, 1] * total[...], m, i, patch_ref, probe_ref, term_ref, sent_ref, tables)
        return carry

    lax.fori_loop(0, half, homeward, 0, unroll=UNROLL)


def second_kernel(
    where_ref, corrected_ref, patch_ref, term_ref, probe_ref, across, down_t, lanes_ref, rows_ref,
    kept_ref, rows0, rows1, rows2, rows3, term, frame,
):
    pattern = patch_ref.shape[1]
    half = corrected_ref.shape[0]
    row_at, core, row_class, turn = where_ref[0], where_ref[1], where_ref[2], where_ref[3]
    lanes, rows = twiddles(lanes_ref, rows_ref)
    tables = (down_t[...], across[...], lanes, rows)
    term[...] = term_ref[...]

    def homeward(i, carry):
        gradients(
            corrected_ref[i, 0],
            corrected_ref[i, 1],
            core * half + (turn ^ i),
            i,
            patch_ref,
            probe_ref,
            term,
            kept_ref,
            tables,
        )
        return carry

    lax.fori_loop(0, half, homeward, 0, unroll=UNROLL)
    block = row_at // ROW_BLOCK
    shift = row_at % ROW_BLOCK
    count = frame.shape[1]
    for channel in range(2):
        padded = jnp.concatenate([term[channel], jnp.zeros((ROW_BLOCK, pattern), F32)], axis=0)
        frame[channel, : count - 3] = pltpu.roll(padded, shift, 0).reshape(count - 3, ROW_BLOCK, pattern)
        frame[channel, count - 3 :] = jnp.zeros((3, ROW_BLOCK, pattern), F32)
    for d, out in enumerate((rows0, rows1, rows2, rows3)):
        first = ((row_class ^ d) + GROUPS - block % GROUPS) % GROUPS
        for i in range(count // GROUPS):
            out[:, i] = frame[:, first + GROUPS * i]


def whole(space=pltpu.VMEM):
    return pl.BlockSpec(memory_space=space)


UNROLL = 4


def first_call(where, pieces, probe, amplitude, tables):
    modes, _, pattern, _ = probe.shape
    half = (modes // 2, 2, pattern, pattern)
    shapes = [half, half, (2, pattern, pattern), (2, pattern, pattern)]
    return pl.pallas_call(
        first_kernel,
        out_shape=[jax.ShapeDtypeStruct(s, F32) for s in shapes],
        in_specs=[whole(pltpu.SMEM)] + [whole()] * 12,
        out_specs=[whole()] * 4,
        scratch_shapes=[
            pltpu.VMEM((2, pattern // ROW_BLOCK + GROUPS, ROW_BLOCK, pattern), F32),
            pltpu.VMEM((modes, 2, pattern, pattern), F32),
            pltpu.VMEM((pattern, pattern), F32),
        ],
        compiler_params=pltpu.CompilerParams(vmem_limit_bytes=VMEM_LIMIT),
        name="outward",
    )(where, *pieces, probe, amplitude, *tables)


def second_call(where, corrected, patch, term, probe, tables):
    down, across, down_t, across_t, lanes, rows = tables
    pattern = patch.shape[1]
    blocks = pattern // ROW_BLOCK + GROUPS
    piece = (2, blocks // GROUPS, ROW_BLOCK, pattern)
    shapes = [corrected.shape] + [piece] * GROUPS
    return pl.pallas_call(
        second_kernel,
        out_shape=[jax.ShapeDtypeStruct(s, F32) for s in shapes],
        in_specs=[whole(pltpu.SMEM)] + [whole()] * 8,
        out_specs=[whole()] * 5,
        scratch_shapes=[
            pltpu.VMEM((2, pattern, pattern), F32),
            pltpu.VMEM((2, blocks, ROW_BLOCK, pattern), F32),
        ],
        compiler_params=pltpu.CompilerParams(vmem_limit_bytes=VMEM_LIMIT),
        name="homeward",
    )(where, corrected, patch, term, probe, across, down_t, lanes, rows)


def class_start(spot, row_class):
    block = spot[0] // ROW_BLOCK
    start = (block + (row_class + GROUPS - block % GROUPS) % GROUPS) // GROUPS
    return pl.multiple_of(start * ROW_BLOCK, ROW_BLOCK)


def cut_kernel(
    class_ref, spot0, spot1, spot2, spot3, tile_ref, right_ref, low_ref, corner_ref, rows0, rows1, rows2, rows3, owned
):
    row_class = class_ref[0]
    _, blocks, _, _, side = tile_ref.shape
    inside = blocks * ROW_BLOCK
    _, outside, _ = low_ref.shape
    for i in range(blocks):
        owned[:, ROW_BLOCK * i : ROW_BLOCK * (i + 1), :side] = tile_ref[:, i, row_class]
    owned[:, :inside, side:] = right_ref[...]
    owned[:, inside : inside + outside, :side] = low_ref[...]
    owned[:, inside : inside + outside, side:] = corner_ref[...]
    owned[:, inside + outside :] = jnp.zeros((2, ROW_BLOCK, owned.shape[2]), F32)
    for spot, rows in ((spot0, rows0), (spot1, rows1), (spot2, rows2), (spot3, rows3)):
        _, count, _, width = rows.shape
        col_at = spot[1]
        down = pl.ds(class_start(spot, row_class), count * ROW_BLOCK)
        across = pl.ds(pl.multiple_of(col_at // 128 * 128, 128), width + 128)
        for channel in range(2):
            wide = pltpu.roll(owned[channel, down, across], (width + 128 - col_at % 128) % (width + 128), 1)
            rows[channel] = wide[:, :width].reshape(count, ROW_BLOCK, width)


def cut_call(row_class, spots, tile, right, low, corner):
    _, blocks, _, _, side = tile.shape
    width = right.shape[2]
    piece = (2, (width // ROW_BLOCK + GROUPS) // GROUPS, ROW_BLOCK, width)
    return pl.pallas_call(
        cut_kernel,
        out_shape=[jax.ShapeDtypeStruct(piece, F32)] * GROUPS,
        in_specs=[whole(pltpu.SMEM)] * 5 + [whole()] * 4,
        out_specs=[whole()] * GROUPS,
        scratch_shapes=[pltpu.VMEM((2, (side + width) // GROUPS + ROW_BLOCK, side + width), F32)],
        compiler_params=pltpu.CompilerParams(vmem_limit_bytes=VMEM_LIMIT),
        name="cut",
    )(row_class, *spots, tile, right, low, corner)


def place_kernel(class_ref, spot0, spot1, spot2, spot3, rows0, rows1, rows2, rows3, body_ref, margin_ref, owned):
    row_class = class_ref[0]
    owned[...] = jnp.zeros_like(owned)
    for spot, rows in ((spot0, rows0), (spot1, rows1), (spot2, rows2), (spot3, rows3)):
        _, count, _, width = rows.shape
        col_at = spot[1]
        down = pl.ds(class_start(spot, row_class), count * ROW_BLOCK)
        across = pl.ds(pl.multiple_of(col_at // 128 * 128, 128), width + 128)
        for channel in range(2):
            block_rows = rows[channel].reshape(count * ROW_BLOCK, width)
            wide = jnp.concatenate([block_rows, jnp.zeros((count * ROW_BLOCK, 128), F32)], axis=1)
            owned[channel, down, across] += pltpu.roll(wide, col_at % 128, 1)
    height, side = body_ref.shape[1:]
    body_ref[...] = owned[:, :height, :side]
    margin_ref[...] = owned[:, :height, side:]


def place_call(row_class, spots, pieces, side):
    _, count, _, width = pieces[0].shape
    height = (side + width) // GROUPS
    return pl.pallas_call(
        place_kernel,
        out_shape=[jax.ShapeDtypeStruct((2, height, w), F32) for w in (side, width)],
        in_specs=[whole(pltpu.SMEM)] * 5 + [whole()] * 4,
        out_specs=[whole()] * 2,
        scratch_shapes=[pltpu.VMEM((2, height + ROW_BLOCK, side + width), F32)],
        compiler_params=pltpu.CompilerParams(vmem_limit_bytes=VMEM_LIMIT),
        name="place",
    )(row_class, *spots, *pieces)


def join_kernel(class_ref, rows0, rows1, rows2, rows3, out_ref):
    for d, rows in enumerate((rows0, rows1, rows2, rows3)):
        place = class_ref[0] ^ d
        for i in range(out_ref.shape[1]):
            out_ref[:, i, place] = rows[:, ROW_BLOCK * i : ROW_BLOCK * (i + 1)]


def join_call(row_class, pieces):
    _, height, side = pieces[0].shape
    out = pl.pallas_call(
        join_kernel,
        out_shape=jax.ShapeDtypeStruct((2, height // ROW_BLOCK, GROUPS, ROW_BLOCK, side), F32),
        in_specs=[whole(pltpu.SMEM)] + [whole()] * 4,
        out_specs=whole(),
        compiler_params=pltpu.CompilerParams(vmem_limit_bytes=VMEM_LIMIT),
        name="join",
    )(row_class, *pieces)
    return out.reshape(1, 2, height * GROUPS, side)


def fill_kernel(slots, count, where_ref, *refs):
    pieces, out_ref, sems = refs[:count], refs[-2], refs[-1]
    core, turns = where_ref[1], (where_ref[3], where_ref[4])
    half = out_ref.shape[0] // 2
    copies = []
    for piece, homes in zip(pieces, slots):
        for i, (side, d, part) in enumerate(homes):
            target = out_ref.at[half * (core ^ side) + (turns[side] ^ d), part]
            copies.append(pltpu.make_async_copy(piece.at[i], target, sems.at[len(copies)]))
    for copy in copies:
        copy.start()
    for copy in copies:
        copy.wait()


def fill_call(where, pieces, slots, shape, base=None):
    pieces = [piece.reshape(-1, *shape[2:]) for piece in pieces]
    given = [] if base is None else [base]
    return pl.pallas_call(
        functools.partial(fill_kernel, slots, len(pieces)),
        out_shape=jax.ShapeDtypeStruct(shape, F32),
        in_specs=[whole(pltpu.SMEM)] + [whole()] * len(pieces) + [whole(pl.ANY)] * len(given),
        out_specs=whole(pl.ANY),
        scratch_shapes=[pltpu.SemaphoreType.DMA((sum(len(homes) for homes in slots),))],
        input_output_aliases={1 + len(pieces): 0} if given else {},
        compiler_params=pltpu.CompilerParams(vmem_limit_bytes=VMEM_LIMIT),
        name="fill",
    )(where, *pieces, *given)


TILE_COLS = 4
AXES = ("y", "zh", "x", "core", "zl")
SIZES = (4, 2, 4, 2, 4)
TILE_AXES = AXES[:4]


def mirrored(tile, group):
    z_hi = tile // 8 % 2
    return group if z_hi == 0 else GROUPS - 1 - group


def across_columns(block, step):
    route = [(t, t + step) for t in range(64) if 0 <= t % TILE_COLS + step < TILE_COLS]
    return lax.ppermute(block, TILE_AXES, route)


def across_rows(block, step, columns=0):
    route = []
    for t in range(64):
        u = t + step * TILE_COLS + columns
        if 0 <= u < 64 and 0 <= t % TILE_COLS + columns < TILE_COLS:
            for k in range(GROUPS):
                route.append((t * GROUPS + mirrored(t, k), u * GROUPS + mirrored(u, k)))
    return lax.ppermute(block, AXES, route)


def among(block, axis, distance):
    n = lax.axis_size(axis)
    return lax.ppermute(block, axis, [(i, i ^ distance) for i in range(n)])


def exchange(block, distance, stage):
    route = []
    for y, zh, x, core, zl in np.ndindex(*SIZES):
        to = (y, zh, x ^ distance, core, zl) if core == stage else (y ^ distance, zh, x, core, zl)
        route.append((int(np.ravel_multi_index((y, zh, x, core, zl), SIZES)), int(np.ravel_multi_index(to, SIZES))))
    return lax.ppermute(block, AXES, route)


def opposite(block):
    route = []
    for y, zh, x, core, zl in np.ndindex(*SIZES):
        to = (y, 1 - zh, x, core, GROUPS - 1 - zl)
        route.append((int(np.ravel_multi_index((y, zh, x, core, zl), SIZES)), int(np.ravel_multi_index(to, SIZES))))
    return lax.ppermute(block, AXES, route)


def exchanged(pieces, stage):
    return [exchange(pieces[d], d, stage) for d in (1, 2, 3)]


def swapped(blocks):
    ranks = np.arange(math.prod(SIZES)).reshape(SIZES)
    groups = [ranks[y, zh, x, core, :: 1 - 2 * zh].tolist() for y, zh, x, core in np.ndindex(*SIZES[:4])]
    return lax.all_to_all(blocks, AXES, 0, 0, axis_index_groups=groups, tiled=True)


def tied(*groups):
    return lax.optimization_barrier(tuple(groups))


def by_place(pieces, me):
    one, two = me % 2 == 1, me // 2 == 1
    pairs = [(jnp.where(one, b, a), jnp.where(one, a, b)) for a, b in (pieces[:2], pieces[2:])]
    low = [jnp.where(two, q, p) for p, q in zip(*pairs)]
    high = [jnp.where(two, p, q) for p, q in zip(*pairs)]
    return jnp.concatenate(low + high)


def total_of(pieces):
    return (pieces[0] + pieces[1]) + (pieces[2] + pieces[3])


def by_parity(amplitude):
    pattern = amplitude.shape[0]
    order = np.concatenate([np.arange(0, pattern, 2), np.arange(1, pattern, 2)])
    table = jnp.asarray(np.eye(pattern, dtype=np.float32)[order])
    exact = lax.Precision.HIGHEST
    return jnp.dot(jnp.dot(table, amplitude, precision=exact), table.T, precision=exact)


def shards(object_tiles, probe, offsets, amplitude):
    own_tile = object_tiles[0]
    pattern = probe.shape[-1]
    tile_side = own_tile.shape[-1]
    place = offsets[0, 0]
    x, y, core, z_hi, z_lo = (lax.axis_index(axis) for axis in ("x", "y", "core", "zh", "zl"))
    row_class = jnp.where(z_hi == 0, z_lo, GROUPS - 1 - z_lo)
    turn, next_turn = jnp.where(core == 0, x, y), jnp.where(core == 0, y, x)
    where = jnp.stack([place[0], core, row_class, turn, next_turn]).astype(jnp.int32)
    own_class = where[2:3]
    tables = [jnp.asarray(table) for table in dft_tables(pattern)]

    blocks = own_tile.reshape(2, -1, GROUPS, ROW_BLOCK, tile_side)
    class_rows = lax.dynamic_index_in_dim(blocks, row_class, 2, keepdims=False).reshape(2, -1, tile_side)
    outside = pattern // GROUPS
    low = across_rows(class_rows[:, :outside], -1)
    corner = across_rows(class_rows[:, :outside, :pattern], -1, -1)
    right = across_columns(class_rows[:, :, :pattern], -1)
    target, place_later = tied(by_parity(amplitude[0, 0]), place)
    spots = [place] + [among(place_later, "zl", d) for d in (1, 2, 3)]
    rows = list(cut_call(own_class, spots, blocks, right, low, corner))
    rows = rows[:1] + [among(rows[d], "zl", d) for d in (1, 2, 3)]

    sent, corrected, patch, term = first_call(where, rows, probe, target, tables)
    arrived = among(sent, "core", 1)
    kept, *rows = second_call(where, corrected, patch, term, probe, tables)

    pieces = [(kept[d] + arrived[d]).reshape(-1, pattern) for d in range(4)]
    pieces, rows = tied(pieces, rows)
    pieces = pieces[:1] + exchanged(pieces, 0)
    rows = rows[:1] + [among(rows[d], "zl", d) for d in (1, 2, 3)]
    mine = total_of(pieces).reshape(4, -1, pattern)
    body, margin = place_call(own_class, spots, rows, tile_side)
    inside = tile_side // GROUPS

    pieces = [lax.dynamic_index_in_dim(mine, next_turn ^ d, 0, keepdims=False) for d in range(4)]
    pieces, margin = tied(pieces, margin)
    body = body.at[:, :, :pattern].add(across_columns(margin, 1))
    pieces = pieces[:1] + exchanged(pieces, 1)
    mine = total_of(pieces).reshape(8, -1, pattern)

    mine = total_of(pieces).reshape(GROUPS, -1, pattern)
    mine, lower = tied(mine, body[:, inside:])
    from_above = across_rows(lower, 1)
    mine = jnp.sum(swapped(mine), axis=0)
    mine = (mine + opposite(mine)) * (1.0 / math.sqrt(mesh_size()))
    body = body[:, :inside].at[:, :outside].add(from_above)

    mine, body = tied(mine, body)
    second = among(body[0], "zl", 2)
    near = [among(mine, "zl", d) for d in (1, 2, 3)]
    near, second, body = tied(near, second, body)
    later = among(body[1], "zl", 2)
    mine = by_place([mine, *near], row_class)
    near = [exchange(mine, d, 1) for d in (1, 2, 3)]
    near, later = tied(near, later)
    second = jnp.stack([second, later])
    mine = by_place([mine, *near], next_turn)
    mine, pair = tied(mine, jnp.stack([body, second]))
    pair = among(pair, "zl", 1)
    pieces = [mine] + exchanged([mine] * 4, 0)
    homes = [[((side, d, 0), (side, d, 1)) for side in range(2)] for d in range(4)]
    *pieces[2:], pair = tied(*pieces[2:], pair)
    other = [among(piece, "core", 1) for piece in pieces]
    done = [pieces[0], other[0], pieces[1], other[1], pieces[2], pieces[3]]
    grad = fill_call(where, done, homes[0] + homes[1] + homes[2][:1] + homes[3][:1], probe.shape)
    grad = fill_call(where, other[2:], homes[2][1:] + homes[3][1:], probe.shape, grad)
    return (join_call(own_class, [body, pair[0], second, pair[1]]), grad)


def mesh_size():
    return math.prod(SIZES)


def solution(mesh):
    fine = Mesh(mesh.devices.reshape(SIZES), AXES)
    placed = (
        P(TILE_AXES, None, None, None),
        P(),
        P(TILE_AXES, "zl", None),
        P(TILE_AXES, "zl", None, None),
    )
    return jax.shard_map(
        shards,
        mesh=fine,
        in_specs=placed,
        out_specs=(P(TILE_AXES, None, None, None), P()),
        check_vma=False,
    )
```

```python
import functools
import math

import jax
import jax.numpy as jnp
import ml_dtypes
import numpy as np
from jax import lax
from jax.experimental import pallas as pl
from jax.experimental.pallas import tpu as pltpu
from jax.sharding import Mesh, PartitionSpec as P

GROUPS = 4
ROW_BLOCK = 8
BF16 = jnp.bfloat16
F32 = jnp.float32
VMEM_LIMIT = 48 * 1024 * 1024


def split_table(table):
    high = table.astype(ml_dtypes.bfloat16)
    low = (table - high.astype(np.float64)).astype(ml_dtypes.bfloat16)
    return high, low


def dft_tables(pattern):
    half = pattern // 2
    angles = 2.0 * np.pi / half * (np.outer(np.arange(half), np.arange(half)) % half)
    cosine, sine = np.cos(angles) / math.sqrt(pattern), np.sin(angles) / math.sqrt(pattern)
    table = np.block([[cosine, -sine], [sine, cosine]])
    high, low = split_table(table)
    down = np.concatenate([high, high, low], axis=0)
    across = np.concatenate([high, high, low], axis=1)
    turned = [np.ascontiguousarray(part.T) for part in (high, low)]
    down_t = np.concatenate([turned[0], turned[0], turned[1]], axis=0)
    across_t = np.concatenate([turned[0], turned[0], turned[1]], axis=1)
    twist = 2.0 * np.pi / pattern * np.arange(half)
    lanes = np.stack([np.cos(twist), -np.sin(twist)])[:, None, :].astype(np.float32)
    rows = np.ascontiguousarray(
        np.broadcast_to(np.stack([np.cos(twist), -np.sin(twist)])[:, :, None], (2, half, half))
    ).astype(np.float32)
    return down, across, down_t, across_t, lanes, rows


def parts(x):
    high = x.astype(BF16)
    return high, (x - high.astype(F32)).astype(BF16)


def times(x, table):
    high, low = parts(x)
    return jnp.dot(jnp.concatenate([high, low, high], axis=1), table, preferred_element_type=F32)


def under(table, x):
    high, low = parts(x)
    return jnp.dot(table, jnp.concatenate([high, low, high], axis=0), preferred_element_type=F32)


def forward(re, im, down, across_t, lanes, rows):
    h = re.shape[0] // 2
    wr, wi = lanes
    a, b, c, d = re[:, :h], re[:, h:], im[:, :h], im[:, h:]
    p, q = a - b, c - d
    even = times(jnp.concatenate([a + b, c + d], axis=1), down)
    odd = times(jnp.concatenate([p * wr - q * wi, p * wi + q * wr], axis=1), down)
    re = jnp.concatenate([even[:, :h], odd[:, :h]], axis=1)
    im = jnp.concatenate([even[:, h:], odd[:, h:]], axis=1)
    wr, wi = rows
    a, b, c, d = re[:h], re[h:], im[:h], im[h:]
    p, q = a - b, c - d
    even = under(across_t, jnp.concatenate([a + b, c + d], axis=0))
    odd = under(across_t, jnp.concatenate([p * wr - q * wi, p * wi + q * wr], axis=0))
    return jnp.concatenate([even[:h], odd[:h]], axis=0), jnp.concatenate([even[h:], odd[h:]], axis=0)


def backward(re, im, down_t, across, lanes, rows):
    h = re.shape[0] // 2
    wr, wi = rows
    even = under(across, jnp.concatenate([re[:h], im[:h]], axis=0))
    odd = under(across, jnp.concatenate([re[h:], im[h:]], axis=0))
    p, q = odd[:h], odd[h:]
    p, q = p * wr + q * wi, q * wr - p * wi
    re = jnp.concatenate([even[:h] + p, even[:h] - p], axis=0)
    im = jnp.concatenate([even[h:] + q, even[h:] - q], axis=0)
    wr, wi = lanes
    even = times(jnp.concatenate([re[:, :h], im[:, :h]], axis=1), down_t)
    odd = times(jnp.concatenate([re[:, h:], im[:, h:]], axis=1), down_t)
    p, q = odd[:, :h], odd[:, h:]
    p, q = p * wr + q * wi, q * wr - p * wi
    re = jnp.concatenate([even[:, :h] + p, even[:, :h] - p], axis=1)
    im = jnp.concatenate([even[:, h:] + q, even[:, h:] - q], axis=1)
    return re, im


def twiddles(lanes_ref, rows_ref):
    rows = [jnp.concatenate([rows_ref[i], rows_ref[i]], axis=1) for i in range(2)]
    return (lanes_ref[0], lanes_ref[1]), rows


def gradients(re, im, m, i, patch_ref, probe_ref, term, grad_ref, tables):
    re, im = backward(re, im, *tables)
    grad_ref[i, 0] = patch_ref[0] * re + patch_ref[1] * im
    grad_ref[i, 1] = patch_ref[0] * im - patch_ref[1] * re
    probe_re, probe_im = probe_ref[m, 0].astype(F32), probe_ref[m, 1].astype(F32)
    term[0] += probe_re * re + probe_im * im
    term[1] += probe_re * im - probe_im * re


def first_kernel(
    where_ref, rows0, rows1, rows2, rows3, probe_ref, amplitude_ref, down, across, down_t, across_t, lanes_ref, rows_ref,
    sent_ref, corrected_ref, patch_ref, term_ref, frame, far, total,
):
    pattern = amplitude_ref.shape[0]
    modes = probe_ref.shape[0]
    half = modes // 2
    row_at, core, other_turn = where_ref[0], where_ref[1], where_ref[4]
    turn = where_ref[3]
    block, shift = row_at // ROW_BLOCK, row_at % ROW_BLOCK
    count = frame.shape[1]
    for d, rows in enumerate((rows0, rows1, rows2, rows3)):
        first = ((where_ref[2] ^ d) + GROUPS - block % GROUPS) % GROUPS
        for i in range(count // GROUPS):
            frame[:, first + GROUPS * i] = rows[:, i]
    height = pattern + ROW_BLOCK
    for channel in range(2):
        window = frame[channel, : count - 3].reshape(height, pattern)
        patch_ref[channel] = pltpu.roll(window, (height - shift) % height, 0)[:pattern]
    lanes, rows = twiddles(lanes_ref, rows_ref)
    total[...] = jnp.full_like(total, 0.01)

    def outward(m, carry):
        probe_re, probe_im = probe_ref[m, 0].astype(F32), probe_ref[m, 1].astype(F32)
        re = probe_re * patch_ref[0] - probe_im * patch_ref[1]
        im = probe_re * patch_ref[1] + probe_im * patch_ref[0]
        re, im = forward(re, im, down[...], across_t[...], lanes, rows)
        far[m, 0] = re
        far[m, 1] = im
        total[...] += re * re + im * im
        return carry

    lax.fori_loop(0, modes, outward, 0, unroll=2 * UNROLL)
    total[...] = 1.0 - amplitude_ref[...] * lax.rsqrt(total[...])
    term_ref[...] = jnp.zeros_like(term_ref)
    tables = (down_t[...], across[...], lanes, rows)

    def homeward(i, carry):
        m = (1 - core) * half + (other_turn ^ i)
        kept = core * half + (turn ^ i)
        corrected_ref[i, 0] = far[kept, 0] * total[...]
        corrected_ref[i, 1] = far[kept, 1] * total[...]
        gradients(far[m, 0] * total[...], far[m, 1] * total[...], m, i, patch_ref, probe_ref, term_ref, sent_ref, tables)
        return carry

    lax.fori_loop(0, half, homeward, 0, unroll=UNROLL)


def second_kernel(
    where_ref, corrected_ref, patch_ref, term_ref, probe_ref, across, down_t, lanes_ref, rows_ref,
    kept_ref, rows0, rows1, rows2, rows3, term, frame,
):
    pattern = patch_ref.shape[1]
    half = corrected_ref.shape[0]
    row_at, core, row_class, turn = where_ref[0], where_ref[1], where_ref[2], where_ref[3]
    lanes, rows = twiddles(lanes_ref, rows_ref)
    tables = (down_t[...], across[...], lanes, rows)
    term[...] = term_ref[...]

    def homeward(i, carry):
        gradients(
            corrected_ref[i, 0],
            corrected_ref[i, 1],
            core * half + (turn ^ i),
            i,
            patch_ref,
            probe_ref,
            term,
            kept_ref,
            tables,
        )
        return carry

    lax.fori_loop(0, half, homeward, 0, unroll=UNROLL)
    block = row_at // ROW_BLOCK
    shift = row_at % ROW_BLOCK
    count = frame.shape[1]
    for channel in range(2):
        padded = jnp.concatenate([term[channel], jnp.zeros((ROW_BLOCK, pattern), F32)], axis=0)
        frame[channel, : count - 3] = pltpu.roll(padded, shift, 0).reshape(count - 3, ROW_BLOCK, pattern)
        frame[channel, count - 3 :] = jnp.zeros((3, ROW_BLOCK, pattern), F32)
    for d, out in enumerate((rows0, rows1, rows2, rows3)):
        first = ((row_class ^ d) + GROUPS - block % GROUPS) % GROUPS
        for i in range(count // GROUPS):
            out[:, i] = frame[:, first + GROUPS * i]


def whole(space=pltpu.VMEM):
    return pl.BlockSpec(memory_space=space)


UNROLL = 4


def first_call(where, pieces, probe, amplitude, tables):
    modes, _, pattern, _ = probe.shape
    half = (modes // 2, 2, pattern, pattern)
    shapes = [half, half, (2, pattern, pattern), (2, pattern, pattern)]
    return pl.pallas_call(
        first_kernel,
        out_shape=[jax.ShapeDtypeStruct(s, F32) for s in shapes],
        in_specs=[whole(pltpu.SMEM)] + [whole()] * 12,
        out_specs=[whole()] * 4,
        scratch_shapes=[
            pltpu.VMEM((2, pattern // ROW_BLOCK + GROUPS, ROW_BLOCK, pattern), F32),
            pltpu.VMEM((modes, 2, pattern, pattern), F32),
            pltpu.VMEM((pattern, pattern), F32),
        ],
        compiler_params=pltpu.CompilerParams(vmem_limit_bytes=VMEM_LIMIT),
        name="outward",
    )(where, *pieces, probe, amplitude, *tables)


def second_call(where, corrected, patch, term, probe, tables):
    down, across, down_t, across_t, lanes, rows = tables
    pattern = patch.shape[1]
    blocks = pattern // ROW_BLOCK + GROUPS
    piece = (2, blocks // GROUPS, ROW_BLOCK, pattern)
    shapes = [corrected.shape] + [piece] * GROUPS
    return pl.pallas_call(
        second_kernel,
        out_shape=[jax.ShapeDtypeStruct(s, F32) for s in shapes],
        in_specs=[whole(pltpu.SMEM)] + [whole()] * 8,
        out_specs=[whole()] * 5,
        scratch_shapes=[
            pltpu.VMEM((2, pattern, pattern), F32),
            pltpu.VMEM((2, blocks, ROW_BLOCK, pattern), F32),
        ],
        compiler_params=pltpu.CompilerParams(vmem_limit_bytes=VMEM_LIMIT),
        name="homeward",
    )(where, corrected, patch, term, probe, across, down_t, lanes, rows)


def class_start(spot, row_class):
    block = spot[0] // ROW_BLOCK
    start = (block + (row_class + GROUPS - block % GROUPS) % GROUPS) // GROUPS
    return pl.multiple_of(start * ROW_BLOCK, ROW_BLOCK)


def cut_kernel(
    class_ref, spot0, spot1, spot2, spot3, tile_ref, right_ref, low_ref, corner_ref, rows0, rows1, rows2, rows3, owned
):
    row_class = class_ref[0]
    _, blocks, _, _, side = tile_ref.shape
    inside = blocks * ROW_BLOCK
    _, outside, _ = low_ref.shape
    for i in range(blocks):
        owned[:, ROW_BLOCK * i : ROW_BLOCK * (i + 1), :side] = tile_ref[:, i, row_class]
    owned[:, :inside, side:] = right_ref[...]
    owned[:, inside : inside + outside, :side] = low_ref[...]
    owned[:, inside : inside + outside, side:] = corner_ref[...]
    owned[:, inside + outside :] = jnp.zeros((2, ROW_BLOCK, owned.shape[2]), F32)
    for spot, rows in ((spot0, rows0), (spot1, rows1), (spot2, rows2), (spot3, rows3)):
        _, count, _, width = rows.shape
        col_at = spot[1]
        down = pl.ds(class_start(spot, row_class), count * ROW_BLOCK)
        across = pl.ds(pl.multiple_of(col_at // 128 * 128, 128), width + 128)
        for channel in range(2):
            wide = pltpu.roll(owned[channel, down, across], (width + 128 - col_at % 128) % (width + 128), 1)
            rows[channel] = wide[:, :width].reshape(count, ROW_BLOCK, width)


def cut_call(row_class, spots, tile, right, low, corner):
    _, blocks, _, _, side = tile.shape
    width = right.shape[2]
    piece = (2, (width // ROW_BLOCK + GROUPS) // GROUPS, ROW_BLOCK, width)
    return pl.pallas_call(
        cut_kernel,
        out_shape=[jax.ShapeDtypeStruct(piece, F32)] * GROUPS,
        in_specs=[whole(pltpu.SMEM)] * 5 + [whole()] * 4,
        out_specs=[whole()] * GROUPS,
        scratch_shapes=[pltpu.VMEM((2, (side + width) // GROUPS + ROW_BLOCK, side + width), F32)],
        compiler_params=pltpu.CompilerParams(vmem_limit_bytes=VMEM_LIMIT),
        name="cut",
    )(row_class, *spots, tile, right, low, corner)


def place_kernel(class_ref, spot0, spot1, spot2, spot3, rows0, rows1, rows2, rows3, body_ref, margin_ref, owned):
    row_class = class_ref[0]
    owned[...] = jnp.zeros_like(owned)
    for spot, rows in ((spot0, rows0), (spot1, rows1), (spot2, rows2), (spot3, rows3)):
        _, count, _, width = rows.shape
        col_at = spot[1]
        down = pl.ds(class_start(spot, row_class), count * ROW_BLOCK)
        across = pl.ds(pl.multiple_of(col_at // 128 * 128, 128), width + 128)
        for channel in range(2):
            block_rows = rows[channel].reshape(count * ROW_BLOCK, width)
            wide = jnp.concatenate([block_rows, jnp.zeros((count * ROW_BLOCK, 128), F32)], axis=1)
            owned[channel, down, across] += pltpu.roll(wide, col_at % 128, 1)
    height, side = body_ref.shape[1:]
    body_ref[...] = owned[:, :height, :side]
    margin_ref[...] = owned[:, :height, side:]


def place_call(row_class, spots, pieces, side):
    _, count, _, width = pieces[0].shape
    height = (side + width) // GROUPS
    return pl.pallas_call(
        place_kernel,
        out_shape=[jax.ShapeDtypeStruct((2, height, w), F32) for w in (side, width)],
        in_specs=[whole(pltpu.SMEM)] * 5 + [whole()] * 4,
        out_specs=[whole()] * 2,
        scratch_shapes=[pltpu.VMEM((2, height + ROW_BLOCK, side + width), F32)],
        compiler_params=pltpu.CompilerParams(vmem_limit_bytes=VMEM_LIMIT),
        name="place",
    )(row_class, *spots, *pieces)


def join_kernel(class_ref, rows0, rows1, rows2, rows3, out_ref):
    for d, rows in enumerate((rows0, rows1, rows2, rows3)):
        place = class_ref[0] ^ d
        for i in range(out_ref.shape[1]):
            out_ref[:, i, place] = rows[:, ROW_BLOCK * i : ROW_BLOCK * (i + 1)]


def join_call(row_class, pieces):
    _, height, side = pieces[0].shape
    out = pl.pallas_call(
        join_kernel,
        out_shape=jax.ShapeDtypeStruct((2, height // ROW_BLOCK, GROUPS, ROW_BLOCK, side), F32),
        in_specs=[whole(pltpu.SMEM)] + [whole()] * 4,
        out_specs=whole(),
        compiler_params=pltpu.CompilerParams(vmem_limit_bytes=VMEM_LIMIT),
        name="join",
    )(row_class, *pieces)
    return out.reshape(1, 2, height * GROUPS, side)


def fill_kernel(slots, count, where_ref, *refs):
    pieces, out_ref, sems = refs[:count], refs[-2], refs[-1]
    core, turns = where_ref[1], (where_ref[3], where_ref[4])
    half = out_ref.shape[0] // 2
    copies = []
    for piece, homes in zip(pieces, slots):
        for i, (side, d, part) in enumerate(homes):
            target = out_ref.at[half * (core ^ side) + (turns[side] ^ d), part]
            copies.append(pltpu.make_async_copy(piece.at[i], target, sems.at[len(copies)]))
    for copy in copies:
        copy.start()
    for copy in copies:
        copy.wait()


def fill_call(where, pieces, slots, shape, base=None):
    pieces = [piece.reshape(-1, *shape[2:]) for piece in pieces]
    given = [] if base is None else [base]
    return pl.pallas_call(
        functools.partial(fill_kernel, slots, len(pieces)),
        out_shape=jax.ShapeDtypeStruct(shape, F32),
        in_specs=[whole(pltpu.SMEM)] + [whole()] * len(pieces) + [whole(pl.ANY)] * len(given),
        out_specs=whole(pl.ANY),
        scratch_shapes=[pltpu.SemaphoreType.DMA((sum(len(homes) for homes in slots),))],
        input_output_aliases={1 + len(pieces): 0} if given else {},
        compiler_params=pltpu.CompilerParams(vmem_limit_bytes=VMEM_LIMIT),
        name="fill",
    )(where, *pieces, *given)


TILE_COLS = 4
AXES = ("y", "zh", "x", "core", "zl")
SIZES = (4, 2, 4, 2, 4)
TILE_AXES = AXES[:4]


def mirrored(tile, group):
    z_hi = tile // 8 % 2
    return group if z_hi == 0 else GROUPS - 1 - group


def across_columns(block, step):
    route = [(t, t + step) for t in range(64) if 0 <= t % TILE_COLS + step < TILE_COLS]
    return lax.ppermute(block, TILE_AXES, route)


def across_rows(block, step, columns=0):
    route = []
    for t in range(64):
        u = t + step * TILE_COLS + columns
        if 0 <= u < 64 and 0 <= t % TILE_COLS + columns < TILE_COLS:
            for k in range(GROUPS):
                route.append((t * GROUPS + mirrored(t, k), u * GROUPS + mirrored(u, k)))
    return lax.ppermute(block, AXES, route)


def among(block, axis, distance):
    n = lax.axis_size(axis)
    return lax.ppermute(block, axis, [(i, i ^ distance) for i in range(n)])


def exchange(block, distance, stage):
    route = []
    for y, zh, x, core, zl in np.ndindex(*SIZES):
        to = (y, zh, x ^ distance, core, zl) if core == stage else (y ^ distance, zh, x, core, zl)
        route.append((int(np.ravel_multi_index((y, zh, x, core, zl), SIZES)), int(np.ravel_multi_index(to, SIZES))))
    return lax.ppermute(block, AXES, route)


def opposite(block):
    route = []
    for y, zh, x, core, zl in np.ndindex(*SIZES):
        to = (y, 1 - zh, x, core, GROUPS - 1 - zl)
        route.append((int(np.ravel_multi_index((y, zh, x, core, zl), SIZES)), int(np.ravel_multi_index(to, SIZES))))
    return lax.ppermute(block, AXES, route)


def exchanged(pieces, stage):
    return [exchange(pieces[d], d, stage) for d in (1, 2, 3)]


def swapped(blocks):
    ranks = np.arange(math.prod(SIZES)).reshape(SIZES)
    groups = [ranks[y, zh, x, core, :: 1 - 2 * zh].tolist() for y, zh, x, core in np.ndindex(*SIZES[:4])]
    return lax.all_to_all(blocks, AXES, 0, 0, axis_index_groups=groups, tiled=True)


def tied(*groups):
    return lax.optimization_barrier(tuple(groups))


def by_place(pieces, me):
    one, two = me % 2 == 1, me // 2 == 1
    pairs = [(jnp.where(one, b, a), jnp.where(one, a, b)) for a, b in (pieces[:2], pieces[2:])]
    low = [jnp.where(two, q, p) for p, q in zip(*pairs)]
    high = [jnp.where(two, p, q) for p, q in zip(*pairs)]
    return jnp.concatenate(low + high)


def total_of(pieces):
    return (pieces[0] + pieces[1]) + (pieces[2] + pieces[3])


def by_parity(amplitude):
    pattern = amplitude.shape[0]
    order = np.concatenate([np.arange(0, pattern, 2), np.arange(1, pattern, 2)])
    table = jnp.asarray(np.eye(pattern, dtype=np.float32)[order])
    exact = lax.Precision.HIGHEST
    return jnp.dot(jnp.dot(table, amplitude, precision=exact), table.T, precision=exact)


def shards(object_tiles, probe, offsets, amplitude):
    own_tile = object_tiles[0]
    pattern = probe.shape[-1]
    tile_side = own_tile.shape[-1]
    place = offsets[0, 0]
    x, y, core, z_hi, z_lo = (lax.axis_index(axis) for axis in ("x", "y", "core", "zh", "zl"))
    row_class = jnp.where(z_hi == 0, z_lo, GROUPS - 1 - z_lo)
    turn, next_turn = jnp.where(core == 0, x, y), jnp.where(core == 0, y, x)
    where = jnp.stack([place[0], core, row_class, turn, next_turn]).astype(jnp.int32)
    own_class = where[2:3]
    tables = [jnp.asarray(table) for table in dft_tables(pattern)]

    blocks = own_tile.reshape(2, -1, GROUPS, ROW_BLOCK, tile_side)
    class_rows = lax.dynamic_index_in_dim(blocks, row_class, 2, keepdims=False).reshape(2, -1, tile_side)
    outside = pattern // GROUPS
    low = across_rows(class_rows[:, :outside], -1)
    corner = across_rows(class_rows[:, :outside, :pattern], -1, -1)
    right = across_columns(class_rows[:, :, :pattern], -1)
    target, place_later = tied(by_parity(amplitude[0, 0]), place)
    spots = [place] + [among(place_later, "zl", d) for d in (1, 2, 3)]
    rows = list(cut_call(own_class, spots, blocks, right, low, corner))
    rows = rows[:1] + [among(rows[d], "zl", d) for d in (1, 2, 3)]

    sent, corrected, patch, term = first_call(where, rows, probe, target, tables)
    arrived = among(sent, "core", 1)
    kept, *rows = second_call(where, corrected, patch, term, probe, tables)

    pieces = [(kept[d] + arrived[d]).reshape(-1, pattern) for d in range(4)]
    pieces, rows = tied(pieces, rows)
    pieces = pieces[:1] + exchanged(pieces, 0)
    rows = rows[:1] + [among(rows[d], "zl", d) for d in (1, 2, 3)]
    mine = total_of(pieces).reshape(4, -1, pattern)
    body, margin = place_call(own_class, spots, rows, tile_side)
    inside = tile_side // GROUPS

    pieces = [lax.dynamic_index_in_dim(mine, next_turn ^ d, 0, keepdims=False) for d in range(4)]
    pieces, margin = tied(pieces, margin)
    body = body.at[:, :, :pattern].add(across_columns(margin, 1))
    pieces = pieces[:1] + exchanged(pieces, 1)
    mine = total_of(pieces).reshape(8, -1, pattern)

    mine = total_of(pieces).reshape(GROUPS, -1, pattern)
    mine, lower = tied(mine, body[:, inside:])
    from_above = across_rows(lower, 1)
    mine = jnp.sum(swapped(mine), axis=0)
    mine = (mine + opposite(mine)) * (1.0 / math.sqrt(mesh_size()))
    body = body[:, :inside].at[:, :outside].add(from_above)

    mine, body = tied(mine, body)
    second = among(body, "zl", 2)
    near = [among(mine, "zl", d) for d in (1, 2, 3)]
    mine = by_place([mine, *near], row_class)
    near = [exchange(mine, d, 1) for d in (1, 2, 3)]
    near, second = tied(near, second)
    mine = by_place([mine, *near], next_turn)
    mine, pair = tied(mine, jnp.stack([body, second]))
    pair = among(pair, "zl", 1)
    pieces = [mine] + exchanged([mine] * 4, 0)
    homes = [[((side, d, 0), (side, d, 1)) for side in range(2)] for d in range(4)]
    *pieces[2:], pair = tied(*pieces[2:], pair)
    other = [among(piece, "core", 1) for piece in pieces]
    done = [pieces[0], other[0], pieces[1], other[1], pieces[2], pieces[3]]
    grad = fill_call(where, done, homes[0] + homes[1] + homes[2][:1] + homes[3][:1], probe.shape)
    grad = fill_call(where, other[2:], homes[2][1:] + homes[3][1:], probe.shape, grad)
    return (join_call(own_class, [body, pair[0], second, pair[1]]), grad)


def mesh_size():
    return math.prod(SIZES)


def solution(mesh):
    fine = Mesh(mesh.devices.reshape(SIZES), AXES)
    placed = (
        P(TILE_AXES, None, None, None),
        P(),
        P(TILE_AXES, "zl", None),
        P(TILE_AXES, "zl", None, None),
    )
    return jax.shard_map(
        shards,
        mesh=fine,
        in_specs=placed,
        out_specs=(P(TILE_AXES, None, None, None), P()),
        check_vma=False,
    )
```
